512 devices in a mesh: blk: 32 (over z, y_lo, core), head: 16 (over y_hi, x).
Axes of the slice: x: 4, y: 8 (y_hi: 4, y_lo: 2; y = y_hi * 2 + y_lo), z: 8, core: 2. Of those that a mesh axis runs over, the one named last changes fastest.
Arguments:
- queries: bfloat16 [4096, 4096], P('blk', 'head'), may hold values from -4 to 4
- keys: bfloat16 [4096, 4096], P('blk', 'head'), may hold values from -4 to 4
- values: bfloat16 [4096, 4096], P('blk', 'head'), may hold values from -6 to 6
- saved_out: bfloat16 [4096, 4096], P('blk', 'head'), may hold values from -6 to 6
- d_layer: bfloat16 [4096, 4096], P('blk', 'head'), may hold values from -6 to 6
- out_weight: bfloat16 [4096, 4096], P('head'), may hold values from -0.09375 to 0.09375
- prefix: int32 [1], replicated, may hold values from 512 to 3071
- block_order: int32 [64], replicated, may hold values from 0 to 63, each once
Outputs:
- grad_queries: bfloat16 [4096, 4096], P('blk', 'head')
- grad_keys: bfloat16 [4096, 4096], P('blk', 'head')
- grad_values: bfloat16 [4096, 4096], P('blk', 'head')
The draws below stay inside these ranges and needn't reach their ends.
Inputs may be any that keep to these rules, and one draw needn't show every extreme that they name: `block_order`: a permutation of the 64 sequence blocks.
All inputs are finite; a program needn't handle non-finite values.
Results may differ from the reference program's by a relative error of at most 0.02.
Values may be sent and summed in bfloat16 or wider, within the bound.
A program may use at most 64 MiB of HBM per device.

```python
import jax
import jax.numpy as jnp
from jax import lax

D = 4096
HD = 256
HEADS = 16
BLK = 64
NBLOCKS = 64
SEQ = 4096


def draw_queries(key, part):
    key = jax.random.fold_in(key, 1)
    base = jax.random.truncated_normal(key, -4.0, 4.0, (SEQ, HEADS * HD))
    return base.astype(jnp.bfloat16)


def draw_keys(key, part):
    key = jax.random.fold_in(key, 2)
    base = jax.random.truncated_normal(key, -4.0, 4.0, (SEQ, HEADS * HD))
    return base.astype(jnp.bfloat16)


def shard_levels(stream_key, extent, pieces, least, largest):
    factor_of, own = 1.0, jax.random.fold_in(stream_key, 6)
    for axis_at, shards_of in pieces:
        heights = jnp.exp(jax.random.uniform(jax.random.fold_in(own, axis_at), (shards_of,), jnp.float32, least / len(pieces), largest / len(pieces)))
        factor_of = factor_of * jnp.repeat(heights, extent[axis_at] // shards_of).reshape([-1 if axis == axis_at else 1 for axis in range(len(extent))])
    return factor_of


def gaussian(key, dims, scale, bound, cuts=(), kind=jnp.bfloat16):
    values = jax.random.normal(key, dims, jnp.float32) * scale
    if len(cuts) > 0:
        values = shard_levels(key, dims, cuts, -0.22, 0.18) * values
    return jnp.clip(values, min=-bound, max=bound).astype(kind)


def setup_inputs(seed: int = 0) -> dict:
    splits = jax.random.split(jax.random.key(seed), 9)
    return {
        "queries": draw_queries(jax.random.fold_in(splits[8], 71), 0),
        "keys": draw_keys(jax.random.fold_in(splits[8], 71), 0),
        "values": gaussian(splits[2], (SEQ, HEADS * HD), 1.0, 6.0, ((0, 32), (1, 16))),
        "saved_out": gaussian(splits[3], (SEQ, HEADS * HD), 1.0, 6.0, ((0, 32), (1, 16))),
        "d_layer": gaussian(splits[4], (SEQ, D), 1.0, 6.0, ((0, 32), (1, 16))),
        "out_weight": gaussian(splits[5], (HEADS * HD, D), D ** -0.5, 0.09375, ((0, 16),)),
        "prefix": jax.random.randint(splits[6], (1,), SEQ // 8, 3 * SEQ // 4).astype(jnp.int32),
        "block_order": jax.random.permutation(splits[7], NBLOCKS).astype(jnp.int32),
    }


def positions(block_order):
    rows = jnp.arange(SEQ, dtype=jnp.int32)
    return block_order[rows // BLK].astype(jnp.int32) * BLK + rows % BLK


def split_heads(array):
    return array.reshape(SEQ, HEADS, HD).transpose(1, 0, 2)


def join_heads(array):
    return array.transpose(1, 0, 2).reshape(SEQ, HEADS * HD)


def reference(queries, keys, values, saved_out, d_layer, out_weight, prefix, block_order):
    score_scale = HD ** -0.5
    position = positions(block_order)
    visible = (position[None, :] <= position[:, None]) | (position[None, :] < prefix[0])
    d_attn = jnp.dot(d_layer, out_weight.T, preferred_element_type=jnp.float32).astype(jnp.bfloat16)

    def one_head(arrays):
        query_h, key_h, value_h, saved_h, grad_h = arrays
        scores = jnp.dot(query_h, key_h.T, preferred_element_type=jnp.float32) * score_scale
        scores = jnp.where(visible, scores, jnp.float32(-1e30))
        row_max = jnp.max(scores, axis=1, keepdims=True)
        row_total = jnp.sum(jnp.where(visible, jnp.exp(scores - row_max), jnp.float32(0.0)), axis=1, keepdims=True)
        lse = row_max + jnp.log(row_total)
        prob = jnp.where(visible, jnp.exp(scores - lse), jnp.float32(0.0))
        delta = jnp.sum(grad_h.astype(jnp.float32) * saved_h.astype(jnp.float32), axis=1, keepdims=True)
        grad_value = jnp.dot(prob.astype(jnp.bfloat16).T, grad_h, preferred_element_type=jnp.float32)
        dprob = jnp.dot(grad_h, value_h.T, preferred_element_type=jnp.float32)
        dscores = (prob * (dprob - delta) * score_scale).astype(jnp.bfloat16)
        grad_query = jnp.dot(dscores, key_h, preferred_element_type=jnp.float32)
        grad_key = jnp.dot(dscores.T, query_h, preferred_element_type=jnp.float32)
        return grad_query.astype(jnp.bfloat16), grad_key.astype(jnp.bfloat16), grad_value.astype(jnp.bfloat16)

    grad_query, grad_key, grad_value = lax.map(one_head, (split_heads(queries), split_heads(keys), split_heads(values), split_heads(saved_out), split_heads(d_attn)))
    return join_heads(grad_query), join_heads(grad_key), join_heads(grad_value)
```

```python
import functools

import jax
import jax.numpy as jnp
from jax import lax
from jax.experimental import pallas as pl
from jax.experimental.pallas import tpu as pltpu
from jax.sharding import PartitionSpec as P

MESH = pl.DeviceIdType.MESH
F32 = jnp.float32
BF16 = jnp.bfloat16

HD = 256
ROWS = 128
HALF = ROWS // 2
NZ = 8
NJ = 4
NH = 4
FLOOR = -1e30
SCALE = HD ** -0.5
MESSAGES = 63


def nt(a, b):
    return lax.dot_general(a, b, (((1,), (1,)), ((), ())), preferred_element_type=F32)


def nn(a, b):
    return lax.dot_general(a, b, (((1,), (0,)), ((), ())), preferred_element_type=F32)


def tn(a, b):
    return lax.dot_general(a, b, (((0,), (0,)), ((), ())), preferred_element_type=F32)


def rows(slot, count=ROWS, first=0):
    return pl.ds(slot * ROWS + first, count)


def kernel(
    prefix_ref,
    order_ref,
    q_hbm,
    k_hbm,
    v_hbm,
    o_hbm,
    d_hbm,
    w_hbm,
    dq_out,
    dk_out,
    dv_out,
    qb,
    kb,
    vb,
    ob,
    dl,
    wb,
    gb,
    st,
    delta,
    score,
    prob,
    ds,
    dv_acc,
    dk_acc,
    dq_acc,
    dv_send,
    dk_send,
    dv_recv,
    dk_recv,
    dq_send,
    dq_recv,
    local_sem,
    send_sem,
    recv_sem,
):
    blk = lax.axis_index("blk")
    head = lax.axis_index("head")
    z, j = lax.div(blk, NJ), lax.rem(blk, NJ)
    yh, x = lax.div(head, NH), lax.rem(head, NH)

    def at_z(step):
        return (lax.rem(z + (step + NZ), NZ) * NJ + j, head)

    def at_y(step):
        return (blk, lax.rem(yh + (step + NH), NH) * NH + x)

    def at_x(step):
        return (blk, yh * NH + lax.rem(x + (step + NH), NH))

    core_peer = (z * NJ + j + 1 - 2 * lax.rem(j, 2), head)
    pair_peer = (z * NJ + j + 2 - 4 * lax.div(j, 2), head)

    loads = {}

    def load(name, src, dst):
        copy = pltpu.make_async_copy(src, dst, local_sem.at[len(loads)])
        copy.start()
        loads[name] = copy

    load("k", k_hbm, kb.at[rows(0)])
    load("q", q_hbm, qb.at[rows(0)])
    load("d", d_hbm, dl.at[rows(0)])
    load("v", v_hbm, vb.at[rows(0)])
    load("w", w_hbm, wb)
    load("o", o_hbm, ob)

    barrier = pltpu.get_barrier_semaphore()
    neighbours = (at_z(1), at_z(-1), at_y(1), at_y(-1), at_x(1), at_x(-1), core_peer, pair_peer)
    for device in neighbours:
        pl.semaphore_signal(barrier, inc=1, device_id=device, device_id_type=MESH)
    pl.semaphore_wait(barrier, len(neighbours))

    sent = {}

    def send(name, src, dst, device):
        index = len(sent)
        copy = pltpu.make_async_remote_copy(
            src_ref=src,
            dst_ref=dst,
            send_sem=send_sem.at[index],
            recv_sem=recv_sem.at[index],
            device_id=device,
            device_id_type=MESH,
        )
        copy.start()
        sent[name] = copy

    def arrived(*names):
        for name in names:
            sent[name].wait_recv()

    def slot_of(dy, dx):
        return (dy % NH) * NH + dx % NH

    def x_start(dy):
        src = dl.at[rows(slot_of(dy, 0))] if dy else d_hbm
        send(("x+", dy), src, dl.at[rows(slot_of(dy, -1))], at_x(1))
        send(("x-", dy), src, dl.at[rows(slot_of(dy, 1))], at_x(-1))

    def x_relay(dy):
        arrived(("x+", dy))
        low = rows(slot_of(dy, -1), HALF)
        send(("xh+", dy), dl.at[low], dl.at[rows(slot_of(dy, 2), HALF)], at_x(1))
        arrived(("x-", dy))
        high = rows(slot_of(dy, 1), HALF, HALF)
        send(("xh-", dy), dl.at[high], dl.at[rows(slot_of(dy, 2), HALF, HALF)], at_x(-1))

    def z_step(kind, hbm, buf, step):
        if step == 0:
            up, down = hbm, hbm
        else:
            arrived((kind, "+", step - 1), (kind, "-", step - 1))
            up, down = buf.at[rows(NZ - step)], buf.at[rows(step)]
        if step < 3:
            send((kind, "+", step), up, buf.at[rows(NZ - 1 - step)], at_z(1))
            send((kind, "-", step), down, buf.at[rows(step + 1)], at_z(-1))
        else:
            low, high = rows(NZ - 3, HALF), rows(3, HALF, HALF)
            send((kind, "+", step), buf.at[low], buf.at[rows(4, HALF)], at_z(1))
            send((kind, "-", step), buf.at[high], buf.at[rows(4, HALF, HALF)], at_z(-1))

    send("y+", d_hbm, dl.at[rows(slot_of(-1, 0))], at_y(1))
    send("y-", d_hbm, dl.at[rows(slot_of(1, 0))], at_y(-1))
    z_step("k", k_hbm, kb, 0)
    x_start(0)
    send("q core", q_hbm, qb.at[rows(1)], core_peer)
    send("q pair", q_hbm, qb.at[rows(2)], pair_peer)
    z_step("v", v_hbm, vb, 0)

    lane = lax.broadcasted_iota(jnp.int32, (1, ROWS), 1)
    sub = lax.broadcasted_iota(jnp.int32, (ROWS, 1), 0)

    def block_positions(index, iota):
        first, second = order_ref[2 * index], order_ref[2 * index + 1]
        return jnp.where(iota < HALF, first * HALF + iota, second * HALF + iota - HALF)

    group = (
        blk,
        z * NJ + j + 1 - 2 * lax.rem(j, 2),
        z * NJ + j + 2 - 4 * lax.div(j, 2),
        z * NJ + 3 - j,
    )
    reach = jnp.concatenate([block_positions(member, lane) for member in group], axis=1)
    reach = jnp.maximum(reach, prefix_ref[0] - 1)

    def score_block(dz):
        scores = nt(kb[rows(dz)], qb[...]) * SCALE
        key_pos = block_positions(lax.rem(z + dz, NZ) * NJ + j, sub)
        scores = jnp.where(key_pos <= reach, scores, FLOOR)
        score[rows(dz)] = scores
        return jnp.max(scores, axis=0, keepdims=True)

    def project(slots):
        total = None
        for dy, dx in slots:
            source = lax.rem(yh + dy % NH, NH) * NH + lax.rem(x + dx % NH, NH)
            columns = pl.ds(pl.multiple_of(source * HD, HD), HD)
            term = nt(dl[rows(slot_of(dy, dx))], wb[:, columns])
            total = term if total is None else total + term
        return total

    x_relay(0)
    z_step("k", k_hbm, kb, 1)
    arrived("q pair")
    send("q on", qb.at[rows(2)], qb.at[rows(3)], core_peer)
    arrived("y+")
    send("yh+", dl.at[rows(slot_of(-1, 0), HALF)], dl.at[rows(slot_of(2, 0), HALF)], at_y(1))
    x_start(3)
    arrived("y-")
    send("yh-", dl.at[rows(slot_of(1, 0), HALF, HALF)], dl.at[rows(slot_of(2, 0), HALF, HALF)], at_y(-1))
    x_start(1)
    z_step("v", v_hbm, vb, 1)
    loads["q"].wait()
    loads["k"].wait()
    arrived("q core", "q on")
    top = score_block(0)
    z_step("k", k_hbm, kb, 2)
    top = jnp.maximum(top, score_block(1))
    top = jnp.maximum(top, score_block(7))
    z_step("v", v_hbm, vb, 2)
    x_relay(3)
    x_relay(1)
    arrived("yh+", "yh-")
    x_start(2)
    z_step("k", k_hbm, kb, 3)
    loads["w"].wait()
    loads["d"].wait()
    arrived(("xh+", 0), ("xh-", 0))
    grad = project([(0, 0), (0, 1), (0, 3), (0, 2)])
    top = jnp.maximum(top, score_block(2))
    top = jnp.maximum(top, score_block(6))
    z_step("v", v_hbm, vb, 3)
    top = jnp.maximum(top, score_block(3))
    top = jnp.maximum(top, score_block(5))
    grad = grad + project([(1, 0), (1, 1), (1, 3), (3, 0), (3, 1), (3, 3)])
    x_relay(2)
    arrived(("k", "+", 3), ("k", "-", 3))
    top = jnp.maximum(top, score_block(4))

    def chunk_sum(dz, total):
        return total + jnp.sum(jnp.exp(score[pl.ds(pl.multiple_of(dz * ROWS, ROWS), ROWS)] - top), axis=0, keepdims=True)

    total = lax.fori_loop(0, NZ, chunk_sum, jnp.zeros((1, NJ * ROWS), F32))

    def swapped(row, distance):
        parts = [row[:, (member ^ distance) * ROWS:((member ^ distance) + 1) * ROWS] for member in range(NJ)]
        return jnp.concatenate(parts, axis=1)

    def exchange(step, name, device, distance, top, total):
        st[2 * step] = jnp.concatenate([jnp.broadcast_to(top, (4, NJ * ROWS)), jnp.broadcast_to(total, (4, NJ * ROWS))], axis=0)
        send(name, st.at[2 * step], st.at[2 * step + 1], device)
        return lambda: merge(step, name, distance, top, total)

    def merge(step, name, distance, top, total):
        arrived(name)
        other_top = swapped(st[2 * step + 1, 0:1], distance)
        other_total = swapped(st[2 * step + 1, 4:5], distance)
        new_top = jnp.maximum(top, other_top)
        return new_top, total * jnp.exp(top - new_top) + other_total * jnp.exp(other_top - new_top)

    finish = exchange(0, "s core", core_peer, 1, top, total)
    arrived(("xh+", 1), ("xh-", 1), ("xh+", 3), ("xh-", 3))
    grad = grad + project([(1, 2), (3, 2), (2, 0), (2, 1), (2, 3)])
    top, total = finish()
    finish = exchange(1, "s pair", pair_peer, 2, top, total)
    loads["o"].wait()

    arrived(("xh+", 2), ("xh-", 2))
    grad = grad + project([(2, 2)])
    grad_low = grad.astype(BF16)
    gb[rows(0)] = grad_low
    send("g core", gb.at[rows(0)], gb.at[rows(1)], core_peer)
    send("g pair", gb.at[rows(0)], gb.at[rows(2)], pair_peer)
    products = grad_low.astype(F32) * ob[...].astype(F32)
    ones = jnp.ones((8, HD), F32)
    delta[0] = lax.dot_general(
        ones, products, (((1,), (1,)), ((), ())), precision=lax.Precision.HIGHEST, preferred_element_type=F32
    )
    send("t core", delta.at[0], delta.at[1], core_peer)
    send("t pair", delta.at[0], delta.at[2], pair_peer)

    top, total = finish()
    log_total = top + jnp.log(total)

    def make_prob(dz, carry):
        here = pl.ds(pl.multiple_of(dz * ROWS, ROWS), ROWS)
        probs = jnp.exp(score[here] - log_total)
        score[here] = probs
        prob[here] = probs.astype(BF16)
        return carry

    lax.fori_loop(0, NZ, make_prob, 0)
    arrived(("v", "+", 3), ("v", "-", 3))
    loads["v"].wait()

    def pair_terms(pair, here, delta_row):
        columns = pl.ds(2 * ROWS * pair, 2 * ROWS)
        grad_pair = gb[columns]
        grad_probs = nt(vb[here], grad_pair)
        grad_scores = (score[here, columns] * (grad_probs - delta_row) * SCALE).astype(BF16)
        ds[here, columns] = grad_scores
        return nn(prob[here, columns], grad_pair), nn(grad_scores, qb[columns])

    arrived("g core", "t core")
    delta_row = jnp.concatenate([delta[0, 0:1], delta[1, 0:1]], axis=1)

    def first_pair(dz, carry):
        here = pl.ds(pl.multiple_of(dz * ROWS, ROWS), ROWS)
        dv, dk = pair_terms(0, here, delta_row)
        dv_acc[here] = dv
        dk_acc[here] = dk
        return carry

    arrived("g pair")
    send("g on", gb.at[rows(2)], gb.at[rows(3)], core_peer)
    arrived("t pair")
    send("t on", delta.at[2], delta.at[3], core_peer)
    lax.fori_loop(0, NZ, first_pair, 0)
    arrived("g on", "t on")
    delta_far = jnp.concatenate([delta[2, 0:1], delta[3, 0:1]], axis=1)

    def second_pair(dz):
        here = rows(dz)
        dv, dk = pair_terms(1, here, delta_far)
        dv_acc[here] = dv_acc[here] + dv
        dk_acc[here] = dk_acc[here] + dk

    def pass_on(kind, acc, out, recv, dz, way, first):
        value = acc[rows(dz)]
        if not first:
            arrived((kind, way, dz))
            value = value + recv[rows(dz)].astype(F32)
        out[rows(dz)] = value.astype(BF16)
        target = (dz - way) % NZ
        landing = target
        if target == 0 and (dz, way) == (1, 1) and kind == "dv":
            landing = 4
        if target == 0 and (dz, way) == (7, -1) and kind == "dk":
            landing = 4
        send((kind, way, target), out.at[rows(dz)], recv.at[rows(landing)], at_z(way))

    dv_pass = functools.partial(pass_on, "dv", dv_acc, dv_send, dv_recv)
    dk_pass = functools.partial(pass_on, "dk", dk_acc, dk_send, dk_recv)

    second_pair(4)
    dv_pass(4, -1, True)
    dk_pass(4, 1, True)
    second_pair(3)
    dv_pass(3, 1, True)
    second_pair(5)
    dk_pass(5, -1, True)
    dv_pass(5, -1, False)
    dk_pass(3, 1, False)
    second_pair(2)
    second_pair(6)
    dv_pass(2, 1, False)
    dk_pass(6, -1, False)
    dv_pass(6, -1, False)
    dk_pass(2, 1, False)
    second_pair(1)
    second_pair(7)
    second_pair(0)
    dv_pass(1, 1, False)
    dk_pass(7, -1, False)
    dv_pass(7, -1, False)
    dk_pass(1, 1, False)

    dq = tn(ds[:, 2 * ROWS:], kb[...])
    dq_send[0:2 * ROWS] = dq.astype(BF16)
    send("dq pair", dq_send.at[pl.ds(0, 2 * ROWS)], dq_recv.at[pl.ds(0, 2 * ROWS)], pair_peer)
    dq_acc[...] = tn(ds[:, :2 * ROWS], kb[...])
    arrived("dq pair")
    dq_send[rows(2)] = (dq_acc[rows(1)] + dq_recv[rows(1)].astype(F32)).astype(BF16)
    send("dq core", dq_send.at[rows(2)], dq_recv.at[rows(2)], core_peer)
    dq = dq_acc[rows(0)] + dq_recv[rows(0)].astype(F32)
    arrived("dq core")
    dq_out[...] = (dq + dq_recv[rows(2)].astype(F32)).astype(BF16)

    def own(kind, acc, recv):
        arrived((kind, 1, 0), (kind, -1, 0))
        return (acc[rows(0)] + recv[rows(0)].astype(F32) + recv[rows(4)].astype(F32)).astype(BF16)

    dv_out[...] = own("dv", dv_acc, dv_recv)
    dk_out[...] = own("dk", dk_acc, dk_recv)
    for copy in sent.values():
        copy.wait_send()


def shards(queries, keys, values, saved_out, d_layer, out_weight, prefix, block_order):
    block = jax.ShapeDtypeStruct((ROWS, HD), BF16)
    anywhere = pl.BlockSpec(memory_space=pl.ANY)
    scalars = pl.BlockSpec(memory_space=pltpu.SMEM)
    vmem = pl.BlockSpec(memory_space=pltpu.VMEM)
    return pl.pallas_call(
        kernel,
        out_shape=(block, block, block),
        in_specs=[scalars, scalars] + [anywhere] * 6,
        out_specs=(vmem, vmem, vmem),
        scratch_shapes=[
            pltpu.VMEM((NJ * ROWS, HD), BF16),
            pltpu.VMEM((NZ * ROWS, HD), BF16),
            pltpu.VMEM((NZ * ROWS, HD), BF16),
            pltpu.VMEM((ROWS, HD), BF16),
            pltpu.VMEM((NH * NH * ROWS, HD), BF16),
            pltpu.VMEM((HD, NH * NH * HD), BF16),
            pltpu.VMEM((NJ * ROWS, HD), BF16),
            pltpu.VMEM((4, 8, NJ * ROWS), F32),
            pltpu.VMEM((NJ, 8, ROWS), F32),
            pltpu.VMEM((NZ * ROWS, NJ * ROWS), F32),
            pltpu.VMEM((NZ * ROWS, NJ * ROWS), BF16),
            pltpu.VMEM((NZ * ROWS, NJ * ROWS), BF16),
            pltpu.VMEM((NZ * ROWS, HD), F32),
            pltpu.VMEM((NZ * ROWS, HD), F32),
            pltpu.VMEM((2 * ROWS, HD), F32),
            pltpu.VMEM((NZ * ROWS, HD), BF16),
            pltpu.VMEM((NZ * ROWS, HD), BF16),
            pltpu.VMEM((NZ * ROWS, HD), BF16),
            pltpu.VMEM((NZ * ROWS, HD), BF16),
            pltpu.VMEM((3 * ROWS, HD), BF16),
            pltpu.VMEM((3 * ROWS, HD), BF16),
            pltpu.SemaphoreType.DMA((6,)),
            pltpu.SemaphoreType.DMA((MESSAGES,)),
            pltpu.SemaphoreType.DMA((MESSAGES,)),
        ],
        compiler_params=pltpu.CompilerParams(
            collective_id=0, has_side_effects=True, vmem_limit_bytes=48 * 1024 * 1024
        ),
    )(prefix, block_order, queries, keys, values, saved_out, d_layer, out_weight)


def solution(mesh):
    tokens = P("blk", "head")
    return jax.shard_map(
        shards,
        mesh=mesh,
        in_specs=(tokens, tokens, tokens, tokens, tokens, P("head", None), P(), P()),
        out_specs=(tokens, tokens, tokens),
        check_vma=False,
    )
```

```python
import functools

import jax
import jax.numpy as jnp
from jax import lax
from jax.experimental import pallas as pl
from jax.experimental.pallas import tpu as pltpu
from jax.sharding import PartitionSpec as P

MESH = pl.DeviceIdType.MESH
F32 = jnp.float32
BF16 = jnp.bfloat16

HD = 256
ROWS = 128
HALF = ROWS // 2
NZ = 8
NJ = 4
NH = 4
FLOOR = -1e30
SCALE = HD ** -0.5
MESSAGES = 87


def nt(a, b):
    return lax.dot_general(a, b, (((1,), (1,)), ((), ())), preferred_element_type=F32)


def nn(a, b):
    return lax.dot_general(a, b, (((1,), (0,)), ((), ())), preferred_element_type=F32)


def tn(a, b):
    return lax.dot_general(a, b, (((0,), (0,)), ((), ())), preferred_element_type=F32)


def rows(slot, count=ROWS, first=0):
    return pl.ds(slot * ROWS + first, count)


def kernel(
    prefix_ref,
    order_hbm,
    q_hbm,
    k_hbm,
    v_hbm,
    o_hbm,
    d_hbm,
    w_hbm,
    dq_out,
    dk_out,
    dv_out,
    order_ref,
    qb,
    kb,
    vb,
    ob,
    dl,
    wb,
    gb,
    tops,
    sums,
    st,
    delta,
    score,
    prob,
    ds,
    dv_acc,
    dk_acc,
    dq_acc,
    dv_send,
    dk_send,
    dv_recv,
    dk_recv,
    dq_send,
    dq_recv,
    local_sem,
    send_sem,
    recv_sem,
):
    blk = lax.axis_index("blk")
    head = lax.axis_index("head")
    z, j = lax.div(blk, NJ), lax.rem(blk, NJ)
    yh, x = lax.div(head, NH), lax.rem(head, NH)

    def at_z(step):
        return (lax.rem(z + (step + NZ), NZ) * NJ + j, head)

    def at_y(step):
        return (blk, lax.rem(yh + (step + NH), NH) * NH + x)

    def at_x(step):
        return (blk, yh * NH + lax.rem(x + (step + NH), NH))

    core_peer = (z * NJ + j + 1 - 2 * lax.rem(j, 2), head)
    pair_peer = (z * NJ + j + 2 - 4 * lax.div(j, 2), head)

    barrier = pltpu.get_barrier_semaphore()
    neighbours = (at_z(1), at_z(-1), at_y(1), at_y(-1), at_x(1), at_x(-1), core_peer, pair_peer)
    for device in neighbours:
        pl.semaphore_signal(barrier, inc=1, device_id=device, device_id_type=MESH)

    loads = {}

    def load(name, src, dst):
        copy = pltpu.make_async_copy(src, dst, local_sem.at[len(loads)])
        copy.start()
        loads[name] = copy

    load("k", k_hbm, kb.at[rows(0)])
    load("q", q_hbm, qb.at[rows(0)])
    load("d", d_hbm, dl.at[rows(0)])
    load("w", w_hbm, wb)
    load("order", order_hbm, order_ref)
    load("v", v_hbm, vb.at[rows(0)])
    load("o", o_hbm, ob)
    pl.semaphore_wait(barrier, len(neighbours))

    sent = {}
    unfinished = []

    def send(name, src, dst, device):
        index = len(sent)
        copy = pltpu.make_async_remote_copy(
            src_ref=src,
            dst_ref=dst,
            send_sem=send_sem.at[index],
            recv_sem=recv_sem.at[index],
            device_id=device,
            device_id_type=MESH,
        )
        copy.start()
        sent[name] = copy
        unfinished.append(copy)

    def arrived(*names):
        for name in names:
            sent[name].wait_recv()

    def settle():
        while unfinished:
            unfinished.pop().wait_send()

    LOW, HIGH = 0, 1

    def half(slot, which):
        return rows(slot, HALF, which * HALF)

    def slot_of(dy, dx):
        return (dy % NH) * NH + dx % NH

    def y_start(which, way):
        send(("y", way, which), d_hbm.at[half(0, which)], dl.at[half(slot_of(-way, 0), which)], at_y(way))

    def y_relay(way):
        which = LOW if way == 1 else HIGH
        arrived(("y", way, which))
        send(("yy", way), dl.at[half(slot_of(-way, 0), which)], dl.at[half(slot_of(2, 0), which)], at_y(way))

    def x_start(dy, which, way):
        block = half(slot_of(dy, 0), which)
        src = dl.at[block] if dy else d_hbm.at[block]
        send(("x", way, dy, which), src, dl.at[half(slot_of(dy, -way), which)], at_x(way))

    def x_both(dy, which):
        x_start(dy, which, 1 if which == LOW else -1)
        x_start(dy, which, -1 if which == LOW else 1)

    def x_relay(dy, way):
        which = LOW if way == 1 else HIGH
        arrived(("x", way, dy, which))
        send(("xx", way, dy), dl.at[half(slot_of(dy, -way), which)], dl.at[half(slot_of(dy, 2), which)], at_x(way))

    def z_step(kind, hbm, buf, step):
        for way in (1, -1):
            near = (-way * step) % NZ
            if step:
                arrived((kind, way, step - 1))
            if step < 3:
                src = buf.at[rows(near)] if step else hbm
                send((kind, way, step), src, buf.at[rows((near - way) % NZ)], at_z(way))
            else:
                which = LOW if way == 1 else HIGH
                send((kind, way, step), buf.at[half(near, which)], buf.at[half(4, which)], at_z(way))

    y_start(LOW, 1)
    y_start(HIGH, -1)
    z_step("k", k_hbm, kb, 0)
    x_both(0, LOW)
    x_both(0, HIGH)
    y_start(HIGH, 1)
    y_start(LOW, -1)
    send("q core", q_hbm, qb.at[rows(1)], core_peer)
    send("q pair", q_hbm, qb.at[rows(2)], pair_peer)
    z_step("v", v_hbm, vb, 0)

    loads["order"].wait()
    lane = lax.broadcasted_iota(jnp.int32, (1, ROWS), 1)
    sub = lax.broadcasted_iota(jnp.int32, (ROWS, 1), 0)

    def block_positions(index, iota):
        first, second = order_ref[2 * index], order_ref[2 * index + 1]
        return jnp.where(iota < HALF, first * HALF + iota, second * HALF + iota - HALF)

    group = (
        blk,
        z * NJ + j + 1 - 2 * lax.rem(j, 2),
        z * NJ + j + 2 - 4 * lax.div(j, 2),
        z * NJ + 3 - j,
    )
    reach = jnp.concatenate([block_positions(member, lane) for member in group], axis=1)
    reach = jnp.maximum(reach, prefix_ref[0] - 1)

    def score_block(dz):
        scores = nt(kb[rows(dz)], qb[...]) * SCALE
        key_pos = block_positions(lax.rem(z + dz, NZ) * NJ + j, sub)
        scores = jnp.where(key_pos <= reach, scores, FLOOR)
        top = jnp.max(scores, axis=0, keepdims=True)
        weights = jnp.exp(scores - top)
        score[rows(dz)] = weights
        tops[dz:dz + 1] = top
        sums[dz:dz + 1] = jnp.sum(weights, axis=0, keepdims=True)

    def project(*slots):
        total = None
        for dy, dx in slots:
            source = lax.rem(yh + dy % NH, NH) * NH + lax.rem(x + dx % NH, NH)
            columns = pl.ds(pl.multiple_of(source * HD, HD), HD)
            term = nt(dl[rows(slot_of(dy, dx))], wb[:, columns])
            total = term if total is None else total + term
        return total

    x_relay(0, 1)
    x_relay(0, -1)
    z_step("k", k_hbm, kb, 1)
    loads["w"].wait()
    loads["d"].wait()
    grad = project((0, 0))
    y_relay(1)
    x_both(3, LOW)
    y_relay(-1)
    x_both(1, HIGH)
    z_step("v", v_hbm, vb, 1)
    arrived(("x", 1, 0, HIGH), ("x", -1, 0, LOW))
    grad = grad + project((0, 1), (0, 3))
    arrived(("y", 1, HIGH))
    x_both(3, HIGH)
    arrived(("y", -1, LOW))
    x_both(1, LOW)
    arrived("q pair")
    send("q on", qb.at[rows(2)], qb.at[rows(3)], core_peer)
    arrived(("xx", 1, 0), ("xx", -1, 0))
    grad = grad + project((0, 2), (1, 0), (3, 0))
    x_relay(3, 1)
    x_relay(1, -1)
    z_step("k", k_hbm, kb, 2)
    loads["q"].wait()
    loads["k"].wait()
    arrived("q core", "q on")
    score_block(0)
    score_block(1)
    arrived(("yy", -1))
    x_both(2, HIGH)
    arrived(("yy", 1))
    x_both(2, LOW)
    x_relay(3, -1)
    x_relay(1, 1)
    z_step("v", v_hbm, vb, 2)
    score_block(7)
    score_block(2)
    score_block(6)
    z_step("k", k_hbm, kb, 3)
    arrived(("x", 1, 1, HIGH), ("x", -1, 1, LOW), ("x", 1, 3, HIGH), ("x", -1, 3, LOW))
    grad = grad + project((1, 1), (1, 3), (3, 1), (3, 3))
    x_relay(2, -1)
    x_relay(2, 1)
    score_block(3)
    score_block(5)
    arrived(("xx", 1, 3), ("xx", -1, 3), ("xx", 1, 1), ("xx", -1, 1))
    grad = grad + project((1, 2), (3, 2), (2, 0))
    z_step("v", v_hbm, vb, 3)
    arrived(("k", 1, 3), ("k", -1, 3))
    score_block(4)

    def swapped(row, distance):
        parts = [row[:, (member ^ distance) * ROWS:((member ^ distance) + 1) * ROWS] for member in range(NJ)]
        return jnp.concatenate(parts, axis=1)

    def offer(step, name, device, top, total):
        st[2 * step] = jnp.concatenate([jnp.broadcast_to(top, (4, NJ * ROWS)), jnp.broadcast_to(total, (4, NJ * ROWS))], axis=0)
        send(name, st.at[2 * step], st.at[2 * step + 1], device)

    def merge(step, name, distance, top, total):
        arrived(name)
        other_top = swapped(st[2 * step + 1, 0:1], distance)
        other_total = swapped(st[2 * step + 1, 4:5], distance)
        new_top = jnp.maximum(top, other_top)
        return new_top, total * jnp.exp(top - new_top) + other_total * jnp.exp(other_top - new_top)

    top = jnp.max(tops[...], axis=0, keepdims=True)
    total = jnp.sum(sums[...] * jnp.exp(tops[...] - top), axis=0, keepdims=True)
    offer(0, "s core", core_peer, top, total)
    arrived(("x", 1, 2, HIGH), ("x", -1, 2, LOW))
    grad = grad + project((2, 1), (2, 3))
    top, total = merge(0, "s core", 1, top, total)
    offer(1, "s pair", pair_peer, top, total)
    arrived(("xx", 1, 2), ("xx", -1, 2))
    grad_low = (grad + project((2, 2))).astype(BF16)
    gb[rows(0)] = grad_low
    send("g pair", gb.at[rows(0)], gb.at[rows(2)], pair_peer)
    send("g core", gb.at[rows(0)], gb.at[rows(1)], core_peer)
    loads["o"].wait()
    products = grad_low.astype(F32) * ob[...].astype(F32)
    ones = jnp.ones((8, HD), F32)
    delta[0] = lax.dot_general(
        ones, products, (((1,), (1,)), ((), ())), precision=lax.Precision.HIGHEST, preferred_element_type=F32
    )
    send("t pair", delta.at[0], delta.at[2], pair_peer)
    send("t core", delta.at[0], delta.at[1], core_peer)

    top, total = merge(1, "s pair", 2, top, total)
    tops[...] = jnp.exp(tops[...] - (top + jnp.log(total)))

    def make_prob(dz):
        probs = score[rows(dz)] * tops[dz:dz + 1]
        score[rows(dz)] = probs
        prob[rows(dz)] = probs.astype(BF16)

    for dz in range(NZ):
        make_prob(dz)
    arrived(("v", 1, 3), ("v", -1, 3))
    loads["v"].wait()

    def pair_terms(pair, here, delta_row):
        columns = pl.ds(2 * ROWS * pair, 2 * ROWS)
        grad_pair = gb[columns]
        grad_probs = nt(vb[here], grad_pair)
        grad_scores = (score[here, columns] * (grad_probs - delta_row) * SCALE).astype(BF16)
        ds[here, columns] = grad_scores
        return nn(prob[here, columns], grad_pair), nn(grad_scores, qb[columns])

    arrived("g core", "t core")
    delta_row = jnp.concatenate([delta[0, 0:1], delta[1, 0:1]], axis=1)

    def first_pair(dz):
        here = rows(dz)
        dv, dk = pair_terms(0, here, delta_row)
        dv_acc[here] = dv
        dk_acc[here] = dk

    for dz in (4, 5, 3, 6):
        first_pair(dz)
    arrived("g pair")
    send("g on", gb.at[rows(2)], gb.at[rows(3)], core_peer)
    arrived("t pair")
    send("t on", delta.at[2], delta.at[3], core_peer)
    for dz in (2, 7, 1, 0):
        first_pair(dz)
    arrived("g on", "t on")
    delta_far = jnp.concatenate([delta[2, 0:1], delta[3, 0:1]], axis=1)

    def second_pair(dz):
        here = rows(dz)
        dv, dk = pair_terms(1, here, delta_far)
        dv_acc[here] = dv_acc[here] + dv
        dk_acc[here] = dk_acc[here] + dk

    def pass_on(kind, acc, out, recv, dz, way, first):
        for which in (LOW, HIGH):
            here = half(dz, which)
            value = acc[here]
            if not first:
                arrived((kind, way, dz, which))
                value = value + recv[here].astype(F32)
            out[here] = value.astype(BF16)
            target = (dz - way) % NZ
            landing = 4 if target == 0 and way == (1 if kind == "dv" else -1) else target
            send((kind, way, target, which), out.at[here], recv.at[half(landing, which)], at_z(way))

    dv_pass = functools.partial(pass_on, "dv", dv_acc, dv_send, dv_recv)
    dk_pass = functools.partial(pass_on, "dk", dk_acc, dk_send, dk_recv)

    def query_term(slot):
        return tn(ds[:, slot * ROWS:(slot + 1) * ROWS], kb[...])

    def query_pair(slot):
        dq_send[rows(slot - 2)] = query_term(slot).astype(BF16)

    second_pair(4)
    dv_pass(4, -1, True)
    dk_pass(4, 1, True)
    second_pair(5)
    dk_pass(5, -1, True)
    second_pair(3)
    dv_pass(3, 1, True)
    second_pair(2)
    second_pair(6)
    dv_pass(5, -1, False)
    dk_pass(3, 1, False)
    second_pair(7)
    second_pair(1)
    dk_pass(6, -1, False)
    dv_pass(2, 1, False)
    second_pair(0)
    query_pair(2)
    dv_pass(6, -1, False)
    dk_pass(2, 1, False)
    query_pair(3)
    send("dq pair", dq_send.at[pl.ds(0, 2 * ROWS)], dq_recv.at[pl.ds(0, 2 * ROWS)], pair_peer)
    dk_pass(7, -1, False)
    dv_pass(1, 1, False)
    dq_acc[rows(1)] = query_term(1)
    dv_pass(7, -1, False)
    dk_pass(1, 1, False)
    dq_acc[rows(0)] = query_term(0)
    arrived("dq pair")
    dq_send[rows(2)] = (dq_acc[rows(1)] + dq_recv[rows(1)].astype(F32)).astype(BF16)
    send("dq core", dq_send.at[rows(2)], dq_recv.at[rows(2)], core_peer)
    dq = dq_acc[rows(0)] + dq_recv[rows(0)].astype(F32)
    settle()
    arrived("dq core")
    dq_out[...] = (dq + dq_recv[rows(2)].astype(F32)).astype(BF16)

    def own(kind, acc, recv, out, which):
        arrived((kind, 1, 0, which), (kind, -1, 0, which))
        ahead, behind = recv[half(0, which)].astype(F32), recv[half(4, which)].astype(F32)
        out[half(0, which)] = (acc[half(0, which)] + ahead + behind).astype(BF16)

    for which in (LOW, HIGH):
        own("dv", dv_acc, dv_recv, dv_out, which)
        own("dk", dk_acc, dk_recv, dk_out, which)


def shards(queries, keys, values, saved_out, d_layer, out_weight, prefix, block_order):
    block = jax.ShapeDtypeStruct((ROWS, HD), BF16)
    anywhere = pl.BlockSpec(memory_space=pl.ANY)
    vmem = pl.BlockSpec(memory_space=pltpu.VMEM)
    operands = (block_order, queries, keys, values, saved_out, d_layer, out_weight)
    return pl.pallas_call(
        kernel,
        out_shape=(block, block, block),
        in_specs=[pl.BlockSpec(memory_space=pltpu.SMEM)] + [anywhere] * 7,
        out_specs=(vmem, vmem, vmem),
        scratch_shapes=[
            pltpu.SMEM((2 * NZ * NJ,), jnp.int32),
            pltpu.VMEM((NJ * ROWS, HD), BF16),
            pltpu.VMEM((NZ * ROWS, HD), BF16),
            pltpu.VMEM((NZ * ROWS, HD), BF16),
            pltpu.VMEM((ROWS, HD), BF16),
            pltpu.VMEM((NH * NH * ROWS, HD), BF16),
            pltpu.VMEM((HD, NH * NH * HD), BF16),
            pltpu.VMEM((NJ * ROWS, HD), BF16),
            pltpu.VMEM((NZ, NJ * ROWS), F32),
            pltpu.VMEM((NZ, NJ * ROWS), F32),
            pltpu.VMEM((4, 8, NJ * ROWS), F32),
            pltpu.VMEM((NJ, 8, ROWS), F32),
            pltpu.VMEM((NZ * ROWS, NJ * ROWS), F32),
            pltpu.VMEM((NZ * ROWS, NJ * ROWS), BF16),
            pltpu.VMEM((NZ * ROWS, NJ * ROWS), BF16),
            pltpu.VMEM((NZ * ROWS, HD), F32),
            pltpu.VMEM((NZ * ROWS, HD), F32),
            pltpu.VMEM((2 * ROWS, HD), F32),
            pltpu.VMEM((NZ * ROWS, HD), BF16),
            pltpu.VMEM((NZ * ROWS, HD), BF16),
            pltpu.VMEM((NZ * ROWS, HD), BF16),
            pltpu.VMEM((NZ * ROWS, HD), BF16),
            pltpu.VMEM((3 * ROWS, HD), BF16),
            pltpu.VMEM((3 * ROWS, HD), BF16),
            pltpu.SemaphoreType.DMA((7,)),
            pltpu.SemaphoreType.DMA((MESSAGES,)),
            pltpu.SemaphoreType.DMA((MESSAGES,)),
        ],
        compiler_params=pltpu.CompilerParams(
            collective_id=0, has_side_effects=True, vmem_limit_bytes=48 * 1024 * 1024
        ),
    )(prefix, *[pltpu.with_memory_space_constraint(operand, pltpu.HBM) for operand in operands])


def solution(mesh):
    tokens = P("blk", "head")
    return jax.shard_map(
        shards,
        mesh=mesh,
        in_specs=(tokens, tokens, tokens, tokens, tokens, P("head", None), P(), P()),
        out_specs=(tokens, tokens, tokens),
        check_vma=False,
    )
```

```python
import functools

import jax
import jax.numpy as jnp
from jax import lax
from jax.experimental import pallas as pl
from jax.experimental.pallas import tpu as pltpu
from jax.sharding import PartitionSpec as P

MESH = pl.DeviceIdType.MESH
F32 = jnp.float32
BF16 = jnp.bfloat16

HD = 256
ROWS = 128
HALF = ROWS // 2
NZ = 8
NJ = 4
NH = 4
FLOOR = -1e30
SCALE = HD ** -0.5
MESSAGES = 100


def nt(a, b):
    return lax.dot_general(a, b, (((1,), (1,)), ((), ())), preferred_element_type=F32)


def nn(a, b):
    return lax.dot_general(a, b, (((1,), (0,)), ((), ())), preferred_element_type=F32)


def tn(a, b):
    return lax.dot_general(a, b, (((0,), (0,)), ((), ())), preferred_element_type=F32)


def rows(slot, count=ROWS, first=0):
    return pl.ds(slot * ROWS + first, count)


def kernel(
    prefix_ref,
    order_hbm,
    q_hbm,
    k_hbm,
    v_hbm,
    o_hbm,
    d_hbm,
    w_hbm,
    out,
    order_ref,
    qb,
    kb,
    vb,
    ob,
    dl,
    wb,
    gb,
    tops,
    sums,
    st,
    delta,
    score,
    prob,
    ds,
    dv_acc,
    dk_acc,
    dq_acc,
    dv_send,
    dk_send,
    dv_recv,
    dk_recv,
    dq_send,
    dq_recv,
    local_sem,
    send_sem,
    recv_sem,
):
    dq_out, dk_out, dv_out = out.at[0], out.at[1], out.at[2]
    blk = lax.axis_index("blk")
    head = lax.axis_index("head")
    z, j = lax.div(blk, NJ), lax.rem(blk, NJ)
    yh, x = lax.div(head, NH), lax.rem(head, NH)

    def at_z(step):
        return (lax.rem(z + (step + NZ), NZ) * NJ + j, head)

    def at_y(step):
        return (blk, lax.rem(yh + (step + NH), NH) * NH + x)

    def at_x(step):
        return (blk, yh * NH + lax.rem(x + (step + NH), NH))

    core_peer = (z * NJ + j + 1 - 2 * lax.rem(j, 2), head)
    pair_peer = (z * NJ + j + 2 - 4 * lax.div(j, 2), head)
    far_peer = (z * NJ + NJ - 1 - j, head)

    barrier = pltpu.get_barrier_semaphore()
    neighbours = (at_z(1), at_z(-1), at_y(1), at_y(-1), at_x(1), at_x(-1), core_peer, pair_peer, far_peer)
    for device in neighbours:
        pl.semaphore_signal(barrier, inc=1, device_id=device, device_id_type=MESH)

    loads = {}

    def load(name, src, dst):
        copy = pltpu.make_async_copy(src, dst, local_sem.at[len(loads)])
        copy.start()
        loads[name] = copy

    load("d", d_hbm, dl.at[rows(0)])
    load("k", k_hbm, kb.at[rows(0)])
    load("q", q_hbm, qb.at[rows(0)])
    load("v", v_hbm, vb.at[rows(0)])
    load("order", order_hbm, order_ref)
    load("w", w_hbm, wb)
    load("o", o_hbm, ob)
    for name in ("d", "k", "q", "v"):
        loads[name].wait()
    pl.semaphore_wait(barrier, len(neighbours))

    sent = {}
    unfinished = []

    def send(name, src, dst, device):
        index = len(sent)
        copy = pltpu.make_async_remote_copy(
            src_ref=src,
            dst_ref=dst,
            send_sem=send_sem.at[index],
            recv_sem=recv_sem.at[index],
            device_id=device,
            device_id_type=MESH,
        )
        copy.start()
        sent[name] = copy
        unfinished.append(copy)

    taken = set()

    def arrived(*names):
        for name in names:
            if name not in taken:
                taken.add(name)
                sent[name].wait_recv()

    def settle():
        while unfinished:
            unfinished.pop().wait_send()

    LOW, HIGH = 0, 1

    def half(slot, which):
        return rows(slot, HALF, which * HALF)

    def slot_of(dy, dx):
        return (dy % NH) * NH + dx % NH

    def y_start(which, way):
        send(("y", way, which), dl.at[half(0, which)], dl.at[half(slot_of(-way, 0), which)], at_y(way))

    def x_start(dy, which, way):
        block = half(slot_of(dy, 0), which)
        send(("x", way, dy, which), dl.at[block], dl.at[half(slot_of(dy, -way), which)], at_x(way))

    def x_both(dy, which):
        x_start(dy, which, 1 if which == LOW else -1)
        x_start(dy, which, -1 if which == LOW else 1)

    def y_relay(way):
        which = LOW if way == 1 else HIGH
        arrived(("y", way, which))
        send(("yy", way), dl.at[half(slot_of(-way, 0), which)], dl.at[half(slot_of(2, 0), which)], at_y(way))
        x_both((-way) % NH, which)

    def y_rest(way):
        which = HIGH if way == 1 else LOW
        arrived(("y", way, which))
        x_both((-way) % NH, which)

    def y_far(way):
        arrived(("yy", way))
        x_both(2, LOW if way == 1 else HIGH)

    def x_relay(dy, way):
        which = LOW if way == 1 else HIGH
        arrived(("x", way, dy, which))
        send(("xx", way, dy), dl.at[half(slot_of(dy, -way), which)], dl.at[half(slot_of(dy, 2), which)], at_x(way))

    stores = {"k": kb, "v": vb}

    def z_send(kind, step, way, which, src):
        near = (-way * step) % NZ
        send((kind, way, step, which), src, stores[kind].at[half((near - way) % NZ, which)], at_z(way))

    def z_start(kind, which):
        own = stores[kind]
        z_send(kind, 0, 1, which, own.at[half(0, which)])
        z_send(kind, 0, -1, 1 - which, own.at[half(0, 1 - which)])

    def z_relay(kind, step, way, which):
        arrived((kind, way, step - 1, which))
        z_send(kind, step, way, which, stores[kind].at[half((-way * step) % NZ, which)])

    y_start(LOW, 1)
    y_start(HIGH, -1)
    z_start("k", LOW)
    x_both(0, LOW)
    x_both(0, HIGH)
    z_start("k", HIGH)
    y_start(HIGH, 1)
    y_start(LOW, -1)
    send("q core", qb.at[rows(0)], qb.at[rows(1)], core_peer)
    z_start("v", LOW)
    z_start("v", HIGH)

    loads["order"].wait()
    lane = lax.broadcasted_iota(jnp.int32, (1, ROWS), 1)
    sub = lax.broadcasted_iota(jnp.int32, (ROWS, 1), 0)

    def block_positions(index, iota):
        first, second = order_ref[2 * index], order_ref[2 * index + 1]
        return jnp.where(iota < HALF, first * HALF + iota, second * HALF + iota - HALF)

    group = (
        blk,
        z * NJ + j + 1 - 2 * lax.rem(j, 2),
        z * NJ + j + 2 - 4 * lax.div(j, 2),
        z * NJ + 3 - j,
    )
    reach = jnp.concatenate([block_positions(member, lane) for member in group], axis=1)
    reach = jnp.maximum(reach, prefix_ref[0] - 1)

    def key_arrival(kind, dz):
        if dz == 0:
            return ()
        if dz == NZ // 2:
            return (kind, 1, 3, LOW), (kind, -1, 3, HIGH)
        way, step = (1, NZ - 1 - dz) if dz > NZ // 2 else (-1, dz - 1)
        return (kind, way, step, LOW), (kind, way, step, HIGH)

    def score_block(dz):
        arrived(*key_arrival("k", dz))
        scores = nt(kb[rows(dz)], qb[...]) * SCALE
        key_pos = block_positions(lax.rem(z + dz, NZ) * NJ + j, sub)
        scores = jnp.where(key_pos <= reach, scores, FLOOR)
        top = jnp.max(scores, axis=0, keepdims=True)
        weights = jnp.exp(scores - top)
        score[rows(dz)] = weights
        tops[dz:dz + 1] = top
        sums[dz:dz + 1] = jnp.sum(weights, axis=0, keepdims=True)

    def arrival(dy, dx):
        if dx == 2:
            return ("xx", 1, dy), ("xx", -1, dy)
        if dx:
            way = 1 if dx == 3 else -1
            return ("x", way, dy, LOW), ("x", way, dy, HIGH)
        return ()

    def project(dy, dx):
        arrived(*arrival(dy, dx))
        source = lax.rem(yh + dy, NH) * NH + lax.rem(x + dx, NH)
        columns = pl.ds(pl.multiple_of(source * HD, HD), HD)
        return nt(dl[rows(slot_of(dy, dx))], wb[:, columns])

    def offer():
        top = jnp.max(tops[...], axis=0, keepdims=True)
        total = jnp.sum(sums[...] * jnp.exp(tops[...] - top), axis=0, keepdims=True)
        wide = (4, NJ * ROWS)
        st[0] = jnp.concatenate([jnp.broadcast_to(top, wide), jnp.broadcast_to(total, wide)], axis=0)
        for distance, device in ((2, pair_peer), (3, far_peer), (1, core_peer)):
            send(("s", distance), st.at[0], st.at[distance], device)

    def statistics(distance, row):
        found = st[distance, row:row + 1]
        parts = [found[:, (member ^ distance) * ROWS:((member ^ distance) + 1) * ROWS] for member in range(NJ)]
        return jnp.concatenate(parts, axis=1)

    def merge():
        arrived(("s", 1), ("s", 2), ("s", 3))
        part_tops = [statistics(distance, 0) for distance in range(NJ)]
        top = functools.reduce(jnp.maximum, part_tops)
        total = sum(statistics(distance, 4) * jnp.exp(part_tops[distance] - top) for distance in range(NJ))
        tops[...] = jnp.exp(tops[...] - (top + jnp.log(total)))

    loads["w"].wait()
    grad = project(0, 0)
    z_relay("k", 1, 1, LOW)
    z_relay("k", 1, -1, HIGH)
    x_relay(0, 1)
    z_relay("k", 1, 1, HIGH)
    z_relay("k", 1, -1, LOW)
    x_relay(0, -1)
    grad = grad + project(0, 3)
    grad = grad + project(0, 1)
    y_relay(1)
    y_relay(-1)
    send("q pair", qb.at[rows(0)], qb.at[rows(2)], pair_peer)
    z_relay("v", 1, 1, LOW)
    z_relay("v", 1, -1, HIGH)
    z_relay("v", 1, 1, HIGH)
    z_relay("v", 1, -1, LOW)
    y_rest(1)
    y_rest(-1)
    z_relay("k", 2, 1, LOW)
    z_relay("k", 2, -1, HIGH)
    grad = grad + project(3, 0)
    grad = grad + project(1, 0)
    grad = grad + project(0, 2)
    z_relay("k", 2, 1, HIGH)
    z_relay("k", 2, -1, LOW)
    x_relay(3, 1)
    z_relay("v", 2, 1, LOW)
    z_relay("v", 2, -1, HIGH)
    arrived("q pair")
    send("q on", qb.at[rows(2)], qb.at[rows(3)], core_peer)
    arrived("q core", "q on")
    score_block(0)
    x_relay(1, -1)
    score_block(1)
    z_relay("v", 2, 1, HIGH)
    z_relay("v", 2, -1, LOW)
    y_far(-1)
    score_block(2)
    x_relay(3, -1)
    y_far(1)
    z_relay("k", 3, 1, LOW)
    z_relay("k", 3, -1, HIGH)
    score_block(6)
    x_relay(1, 1)
    score_block(7)
    grad = grad + project(3, 3)
    grad = grad + project(3, 1)
    grad = grad + project(2, 0)
    z_relay("v", 3, 1, LOW)
    z_relay("v", 3, -1, HIGH)
    grad = grad + project(1, 3)
    grad = grad + project(1, 1)
    score_block(5)
    score_block(3)
    x_relay(2, -1)
    x_relay(2, 1)
    grad = grad + project(2, 3)
    score_block(4)
    offer()
    grad = grad + project(3, 2)
    grad = grad + project(1, 2)
    grad = grad + project(2, 1)
    grad = grad + project(2, 2)
    grad_low = grad.astype(BF16)
    gb[rows(0)] = grad_low
    send("g pair", gb.at[rows(0)], gb.at[rows(2)], pair_peer)
    send("g core", gb.at[rows(0)], gb.at[rows(1)], core_peer)
    loads["o"].wait()
    products = grad_low.astype(F32) * ob[...].astype(F32)
    ones = jnp.ones((8, HD), F32)
    delta[0] = lax.dot_general(
        ones, products, (((1,), (1,)), ((), ())), precision=lax.Precision.HIGHEST, preferred_element_type=F32
    )
    for distance, device in ((2, pair_peer), (3, far_peer), (1, core_peer)):
        send(("t", distance), delta.at[0], delta.at[distance], device)
    merge()

    def make_prob(dz):
        probs = score[rows(dz)] * tops[dz:dz + 1]
        score[rows(dz)] = probs
        prob[rows(dz)] = probs.astype(BF16)

    for dz in range(NZ):
        make_prob(dz)
    for dz in range(NZ):
        arrived(*key_arrival("v", dz))

    def pair_terms(pair, here, delta_row):
        columns = pl.ds(2 * ROWS * pair, 2 * ROWS)
        grad_pair = gb[columns]
        grad_probs = nt(vb[here], grad_pair)
        grad_scores = (score[here, columns] * (grad_probs - delta_row) * SCALE).astype(BF16)
        ds[here, columns] = grad_scores
        return nn(prob[here, columns], grad_pair), nn(grad_scores, qb[columns])

    arrived("g core", ("t", 1))
    delta_row = jnp.concatenate([delta[0, 0:1], delta[1, 0:1]], axis=1)

    def first_pair(dz):
        here = rows(dz)
        dv, dk = pair_terms(0, here, delta_row)
        dv_acc[here] = dv
        dk_acc[here] = dk

    for dz in (4, 5, 3, 6):
        first_pair(dz)
    arrived("g pair")
    send("g on", gb.at[rows(2)], gb.at[rows(3)], core_peer)
    for dz in (2, 7, 1, 0):
        first_pair(dz)
    arrived("g on", ("t", 2), ("t", 3))
    delta_far = jnp.concatenate([delta[2, 0:1], delta[3, 0:1]], axis=1)

    def second_pair(dz):
        here = rows(dz)
        dv, dk = pair_terms(1, here, delta_far)
        dv_acc[here] = dv_acc[here] + dv
        dk_acc[here] = dk_acc[here] + dk

    sums_of = {"dv": (dv_acc, dv_send, dv_recv), "dk": (dk_acc, dk_send, dk_recv)}

    def pass_on(*parts):
        for which in (LOW, HIGH):
            for kind, dz, way, first in parts:
                acc, out, recv = sums_of[kind]
                here = half(dz, which)
                value = acc[here]
                if not first:
                    arrived((kind, way, dz, which))
                    value = value + recv[here].astype(F32)
                out[here] = value.astype(BF16)
                target = (dz - way) % NZ
                landing = 4 if target == 0 and way == (1 if kind == "dv" else -1) else target
                send((kind, way, target, which), out.at[here], recv.at[half(landing, which)], at_z(way))

    def query_term(slot):
        return tn(ds[:, slot * ROWS:(slot + 1) * ROWS], kb[...])

    def query_pair(slot):
        dq_send[rows(slot - 2)] = query_term(slot).astype(BF16)

    second_pair(4)
    pass_on(("dv", 4, -1, True), ("dk", 4, 1, True))
    second_pair(5)
    second_pair(3)
    pass_on(("dk", 5, -1, True), ("dv", 3, 1, True))
    second_pair(2)
    second_pair(6)
    pass_on(("dv", 5, -1, False), ("dk", 3, 1, False))
    second_pair(7)
    second_pair(1)
    pass_on(("dk", 6, -1, False), ("dv", 2, 1, False))
    second_pair(0)
    query_pair(2)
    pass_on(("dv", 6, -1, False), ("dk", 2, 1, False))
    query_pair(3)
    send("dq pair", dq_send.at[pl.ds(0, 2 * ROWS)], dq_recv.at[pl.ds(0, 2 * ROWS)], pair_peer)
    pass_on(("dk", 7, -1, False), ("dv", 1, 1, False))
    dq_acc[rows(1)] = query_term(1)
    pass_on(("dv", 7, -1, False), ("dk", 1, 1, False))
    dq_acc[rows(0)] = query_term(0)
    arrived("dq pair")
    dq_send[rows(2)] = (dq_acc[rows(1)] + dq_recv[rows(1)].astype(F32)).astype(BF16)
    send("dq core", dq_send.at[rows(2)], dq_recv.at[rows(2)], core_peer)
    dq = dq_acc[rows(0)] + dq_recv[rows(0)].astype(F32)
    settle()
    arrived("dq core")
    dq_out[...] = (dq + dq_recv[rows(2)].astype(F32)).astype(BF16)

    def own(kind, acc, recv, out, which):
        arrived((kind, 1, 0, which), (kind, -1, 0, which))
        ahead, behind = recv[half(0, which)].astype(F32), recv[half(4, which)].astype(F32)
        out[half(0, which)] = (acc[half(0, which)] + ahead + behind).astype(BF16)

    for which in (LOW, HIGH):
        own("dv", dv_acc, dv_recv, dv_out, which)
        own("dk", dk_acc, dk_recv, dk_out, which)


def shards(queries, keys, values, saved_out, d_layer, out_weight, prefix, block_order):
    block = jax.ShapeDtypeStruct((ROWS, HD), BF16)
    anywhere = pl.BlockSpec(memory_space=pl.ANY)
    vmem = pl.BlockSpec(memory_space=pltpu.VMEM)
    operands = (block_order, queries, keys, values, saved_out, d_layer, out_weight)
    results = pl.pallas_call(
        kernel,
        out_shape=jax.ShapeDtypeStruct((3, ROWS, HD), BF16),
        in_specs=[pl.BlockSpec(memory_space=pltpu.SMEM)] + [anywhere] * 7,
        out_specs=vmem,
        scratch_shapes=[
            pltpu.SMEM((2 * NZ * NJ,), jnp.int32),
            pltpu.VMEM((NJ * ROWS, HD), BF16),
            pltpu.VMEM((NZ * ROWS, HD), BF16),
            pltpu.VMEM((NZ * ROWS, HD), BF16),
            pltpu.VMEM((ROWS, HD), BF16),
            pltpu.VMEM((NH * NH * ROWS, HD), BF16),
            pltpu.VMEM((HD, NH * NH * HD), BF16),
            pltpu.VMEM((NJ * ROWS, HD), BF16),
            pltpu.VMEM((NZ, NJ * ROWS), F32),
            pltpu.VMEM((NZ, NJ * ROWS), F32),
            pltpu.VMEM((4, 8, NJ * ROWS), F32),
            pltpu.VMEM((NJ, 8, ROWS), F32),
            pltpu.VMEM((NZ * ROWS, NJ * ROWS), F32),
            pltpu.VMEM((NZ * ROWS, NJ * ROWS), BF16),
            pltpu.VMEM((NZ * ROWS, NJ * ROWS), BF16),
            pltpu.VMEM((NZ * ROWS, HD), F32),
            pltpu.VMEM((NZ * ROWS, HD), F32),
            pltpu.VMEM((2 * ROWS, HD), F32),
            pltpu.VMEM((NZ * ROWS, HD), BF16),
            pltpu.VMEM((NZ * ROWS, HD), BF16),
            pltpu.VMEM((NZ * ROWS, HD), BF16),
            pltpu.VMEM((NZ * ROWS, HD), BF16),
            pltpu.VMEM((3 * ROWS, HD), BF16),
            pltpu.VMEM((3 * ROWS, HD), BF16),
            pltpu.SemaphoreType.DMA((7,)),
            pltpu.SemaphoreType.DMA((MESSAGES,)),
            pltpu.SemaphoreType.DMA((MESSAGES,)),
        ],
        compiler_params=pltpu.CompilerParams(
            collective_id=0, has_side_effects=True, vmem_limit_bytes=48 * 1024 * 1024
        ),
    )(prefix, *[pltpu.with_memory_space_constraint(operand, pltpu.HBM) for operand in operands])
    return results[0], results[1], results[2]


def solution(mesh):
    tokens = P("blk", "head")
    return jax.shard_map(
        shards,
        mesh=mesh,
        in_specs=(tokens, tokens, tokens, tokens, tokens, P("head", None), P(), P()),
        out_specs=(tokens, tokens, tokens),
        check_vma=False,
    )
```

```python
import functools

import jax
import jax.numpy as jnp
from jax import lax
from jax.experimental import pallas as pl
from jax.experimental.pallas import tpu as pltpu
from jax.sharding import PartitionSpec as P

MESH = pl.DeviceIdType.MESH
F32 = jnp.float32
BF16 = jnp.bfloat16

HD = 256
ROWS = 128
HALF = ROWS // 2
NZ = 8
NJ = 4
NH = 4
FLOOR = -1e30
SCALE = HD ** -0.5
MESSAGES = 100


def nt(a, b):
    return lax.dot_general(a, b, (((1,), (1,)), ((), ())), preferred_element_type=F32)


def nn(a, b):
    return lax.dot_general(a, b, (((1,), (0,)), ((), ())), preferred_element_type=F32)


def tn(a, b):
    return lax.dot_general(a, b, (((0,), (0,)), ((), ())), preferred_element_type=F32)


def rows(slot, count=ROWS, first=0):
    return pl.ds(slot * ROWS + first, count)


def kernel(
    prefix_ref,
    order_hbm,
    q_hbm,
    k_hbm,
    v_hbm,
    o_hbm,
    d_hbm,
    w_hbm,
    out,
    order_ref,
    qb,
    kb,
    vb,
    ob,
    dl,
    wb,
    gb,
    tops,
    sums,
    st,
    delta,
    score,
    prob,
    ds,
    dv_acc,
    dk_acc,
    dq_acc,
    dv_send,
    dk_send,
    dv_recv,
    dk_recv,
    dq_send,
    dq_recv,
    local_sem,
    send_sem,
    recv_sem,
):
    dq_out, dk_out, dv_out = out.at[0], out.at[1], out.at[2]
    blk = lax.axis_index("blk")
    head = lax.axis_index("head")
    z, j = lax.div(blk, NJ), lax.rem(blk, NJ)
    yh, x = lax.div(head, NH), lax.rem(head, NH)

    def at_z(step):
        return (lax.rem(z + (step + NZ), NZ) * NJ + j, head)

    def at_y(step):
        return (blk, lax.rem(yh + (step + NH), NH) * NH + x)

    def at_x(step):
        return (blk, yh * NH + lax.rem(x + (step + NH), NH))

    core_peer = (z * NJ + j + 1 - 2 * lax.rem(j, 2), head)
    pair_peer = (z * NJ + j + 2 - 4 * lax.div(j, 2), head)
    far_peer = (z * NJ + NJ - 1 - j, head)

    barrier = pltpu.get_barrier_semaphore()
    neighbours = (at_z(1), at_z(-1), at_y(1), at_y(-1), at_x(1), at_x(-1), core_peer, pair_peer, far_peer)
    for device in neighbours:
        pl.semaphore_signal(barrier, inc=1, device_id=device, device_id_type=MESH)

    loads = {}

    def load(name, src, dst):
        copy = pltpu.make_async_copy(src, dst, local_sem.at[len(loads)])
        copy.start()
        loads[name] = copy

    load("d", d_hbm, dl.at[rows(0)])
    load("k", k_hbm, kb.at[rows(0)])
    load("q", q_hbm, qb.at[rows(0)])
    load("v", v_hbm, vb.at[rows(0)])
    load("order", order_hbm, order_ref)
    load("w", w_hbm, wb)
    load("o", o_hbm, ob)
    for name in ("d", "k", "q", "v"):
        loads[name].wait()
    pl.semaphore_wait(barrier, len(neighbours))

    sent = {}
    unfinished = []

    def send(name, src, dst, device):
        index = len(sent)
        copy = pltpu.make_async_remote_copy(
            src_ref=src,
            dst_ref=dst,
            send_sem=send_sem.at[index],
            recv_sem=recv_sem.at[index],
            device_id=device,
            device_id_type=MESH,
        )
        copy.start()
        sent[name] = copy
        unfinished.append(copy)

    taken = set()

    def arrived(*names):
        for name in names:
            if name not in taken:
                taken.add(name)
                sent[name].wait_recv()

    def settle():
        while unfinished:
            unfinished.pop().wait_send()

    LOW, HIGH = 0, 1

    def half(slot, which):
        return rows(slot, HALF, which * HALF)

    def slot_of(dy, dx):
        return (dy % NH) * NH + dx % NH

    def y_start(which, way):
        send(("y", way, which), dl.at[half(0, which)], dl.at[half(slot_of(-way, 0), which)], at_y(way))

    def x_start(dy, which, way):
        block = half(slot_of(dy, 0), which)
        send(("x", way, dy, which), dl.at[block], dl.at[half(slot_of(dy, -way), which)], at_x(way))

    def x_both(dy, which):
        x_start(dy, which, 1 if which == LOW else -1)
        x_start(dy, which, -1 if which == LOW else 1)

    def y_relay(way):
        which = LOW if way == 1 else HIGH
        arrived(("y", way, which))
        send(("yy", way), dl.at[half(slot_of(-way, 0), which)], dl.at[half(slot_of(2, 0), which)], at_y(way))
        x_both((-way) % NH, which)

    def y_rest(way):
        which = HIGH if way == 1 else LOW
        arrived(("y", way, which))
        x_both((-way) % NH, which)

    def y_far(way):
        arrived(("yy", way))
        x_both(2, LOW if way == 1 else HIGH)

    def x_relay(dy, way):
        which = LOW if way == 1 else HIGH
        arrived(("x", way, dy, which))
        send(("xx", way, dy), dl.at[half(slot_of(dy, -way), which)], dl.at[half(slot_of(dy, 2), which)], at_x(way))

    stores = {"k": kb, "v": vb}

    def z_send(kind, step, way, which, src):
        near = (-way * step) % NZ
        send((kind, way, step, which), src, stores[kind].at[half((near - way) % NZ, which)], at_z(way))

    def z_start(kind, which):
        own = stores[kind]
        z_send(kind, 0, 1, which, own.at[half(0, which)])
        z_send(kind, 0, -1, 1 - which, own.at[half(0, 1 - which)])

    def z_relay(kind, step, way, which):
        arrived((kind, way, step - 1, which))
        z_send(kind, step, way, which, stores[kind].at[half((-way * step) % NZ, which)])

    y_start(LOW, 1)
    y_start(HIGH, -1)
    z_start("k", LOW)
    x_both(0, LOW)
    x_both(0, HIGH)
    z_start("k", HIGH)
    y_start(HIGH, 1)
    y_start(LOW, -1)
    send("q core", qb.at[rows(0)], qb.at[rows(1)], core_peer)
    z_start("v", LOW)

    loads["order"].wait()
    lane = lax.broadcasted_iota(jnp.int32, (1, ROWS), 1)
    sub = lax.broadcasted_iota(jnp.int32, (ROWS, 1), 0)

    def block_positions(index, iota):
        first, second = order_ref[2 * index], order_ref[2 * index + 1]
        return jnp.where(iota < HALF, first * HALF + iota, second * HALF + iota - HALF)

    group = (
        blk,
        z * NJ + j + 1 - 2 * lax.rem(j, 2),
        z * NJ + j + 2 - 4 * lax.div(j, 2),
        z * NJ + 3 - j,
    )
    reach = jnp.concatenate([block_positions(member, lane) for member in group], axis=1)
    reach = jnp.maximum(reach, prefix_ref[0] - 1)

    def key_arrival(kind, dz):
        if dz == 0:
            return ()
        if dz == NZ // 2:
            return (kind, 1, 3, LOW), (kind, -1, 3, HIGH)
        way, step = (1, NZ - 1 - dz) if dz > NZ // 2 else (-1, dz - 1)
        return (kind, way, step, LOW), (kind, way, step, HIGH)

    def score_block(dz):
        arrived(*key_arrival("k", dz))
        scores = nt(kb[rows(dz)], qb[...]) * SCALE
        key_pos = block_positions(lax.rem(z + dz, NZ) * NJ + j, sub)
        scores = jnp.where(key_pos <= reach, scores, FLOOR)
        top = jnp.max(scores, axis=0, keepdims=True)
        weights = jnp.exp(scores - top)
        score[rows(dz)] = weights
        tops[dz:dz + 1] = top
        sums[dz:dz + 1] = jnp.sum(weights, axis=0, keepdims=True)

    def arrival(dy, dx):
        if dx == 2:
            return ("xx", 1, dy), ("xx", -1, dy)
        if dx:
            way = 1 if dx == 3 else -1
            return ("x", way, dy, LOW), ("x", way, dy, HIGH)
        return ()

    def project(dy, dx):
        arrived(*arrival(dy, dx))
        source = lax.rem(yh + dy, NH) * NH + lax.rem(x + dx, NH)
        columns = pl.ds(pl.multiple_of(source * HD, HD), HD)
        return nt(dl[rows(slot_of(dy, dx))], wb[:, columns])

    def offer():
        top = jnp.max(tops[...], axis=0, keepdims=True)
        total = jnp.sum(sums[...] * jnp.exp(tops[...] - top), axis=0, keepdims=True)
        wide = (4, NJ * ROWS)
        st[0] = jnp.concatenate([jnp.broadcast_to(top, wide), jnp.broadcast_to(total, wide)], axis=0)
        for distance, device in ((2, pair_peer), (3, far_peer), (1, core_peer)):
            send(("s", distance), st.at[0], st.at[distance], device)

    def statistics(distance, row):
        found = st[distance, row:row + 1]
        parts = [found[:, (member ^ distance) * ROWS:((member ^ distance) + 1) * ROWS] for member in range(NJ)]
        return jnp.concatenate(parts, axis=1)

    def merge():
        arrived(("s", 1), ("s", 2), ("s", 3))
        part_tops = [statistics(distance, 0) for distance in range(NJ)]
        top = functools.reduce(jnp.maximum, part_tops)
        total = sum(statistics(distance, 4) * jnp.exp(part_tops[distance] - top) for distance in range(NJ))
        tops[...] = jnp.exp(tops[...] - (top + jnp.log(total)))

    loads["w"].wait()
    grad = project(0, 0)
    z_relay("k", 1, 1, LOW)
    z_relay("k", 1, -1, HIGH)
    x_relay(0, 1)
    z_relay("k", 1, 1, HIGH)
    z_relay("k", 1, -1, LOW)
    x_relay(0, -1)
    z_start("v", HIGH)
    grad = grad + project(0, 3)
    grad = grad + project(0, 1)
    y_relay(1)
    y_relay(-1)
    send("q pair", qb.at[rows(0)], qb.at[rows(2)], pair_peer)
    z_relay("k", 2, 1, LOW)
    z_relay("k", 2, -1, HIGH)
    y_rest(1)
    y_rest(-1)
    grad = grad + project(3, 0)
    grad = grad + project(1, 0)
    z_relay("k", 2, 1, HIGH)
    z_relay("k", 2, -1, LOW)
    z_relay("v", 1, 1, LOW)
    z_relay("v", 1, -1, HIGH)
    grad = grad + project(0, 2)
    x_relay(3, 1)
    x_relay(1, -1)
    z_relay("k", 3, 1, LOW)
    z_relay("k", 3, -1, HIGH)
    z_relay("v", 1, 1, HIGH)
    z_relay("v", 1, -1, LOW)
    y_far(1)
    y_far(-1)
    grad = grad + project(2, 0)
    grad = grad + project(3, 3)
    x_relay(3, -1)
    grad = grad + project(3, 1)
    arrived("q pair")
    send("q on", qb.at[rows(2)], qb.at[rows(3)], core_peer)
    x_relay(1, 1)
    grad = grad + project(1, 3)
    grad = grad + project(1, 1)
    z_relay("v", 2, 1, LOW)
    z_relay("v", 2, -1, HIGH)
    arrived("q core", "q on")
    score_block(0)
    score_block(1)
    x_relay(2, 1)
    score_block(2)
    z_relay("v", 2, 1, HIGH)
    z_relay("v", 2, -1, LOW)
    score_block(3)
    score_block(5)
    x_relay(2, -1)
    score_block(6)
    z_relay("v", 3, 1, LOW)
    z_relay("v", 3, -1, HIGH)
    score_block(7)
    score_block(4)
    offer()
    grad = grad + project(2, 3)
    grad = grad + project(2, 1)
    grad = grad + project(1, 2)
    grad = grad + project(3, 2)
    grad = grad + project(2, 2)
    grad_low = grad.astype(BF16)
    gb[rows(0)] = grad_low
    send("g pair", gb.at[rows(0)], gb.at[rows(2)], pair_peer)
    send("g core", gb.at[rows(0)], gb.at[rows(1)], core_peer)
    loads["o"].wait()
    products = grad_low.astype(F32) * ob[...].astype(F32)
    ones = jnp.ones((8, HD), F32)
    delta[0] = lax.dot_general(
        ones, products, (((1,), (1,)), ((), ())), precision=lax.Precision.HIGHEST, preferred_element_type=F32
    )
    for distance, device in ((2, pair_peer), (3, far_peer), (1, core_peer)):
        send(("t", distance), delta.at[0], delta.at[distance], device)
    merge()

    def make_prob(dz):
        probs = score[rows(dz)] * tops[dz:dz + 1]
        score[rows(dz)] = probs
        prob[rows(dz)] = probs.astype(BF16)

    for dz in range(NZ):
        make_prob(dz)
    for dz in range(NZ):
        arrived(*key_arrival("v", dz))

    def pair_terms(pair, here, delta_row):
        columns = pl.ds(2 * ROWS * pair, 2 * ROWS)
        grad_pair = gb[columns]
        grad_probs = nt(vb[here], grad_pair)
        grad_scores = (score[here, columns] * (grad_probs - delta_row) * SCALE).astype(BF16)
        ds[here, columns] = grad_scores
        return nn(prob[here, columns], grad_pair), nn(grad_scores, qb[columns])

    arrived("g core", ("t", 1))
    delta_row = jnp.concatenate([delta[0, 0:1], delta[1, 0:1]], axis=1)

    def first_pair(dz):
        here = rows(dz)
        dv, dk = pair_terms(0, here, delta_row)
        dv_acc[here] = dv
        dk_acc[here] = dk

    for dz in (4, 5, 3, 6):
        first_pair(dz)
    arrived("g pair")
    send("g on", gb.at[rows(2)], gb.at[rows(3)], core_peer)
    for dz in (2, 7, 1, 0):
        first_pair(dz)
    arrived("g on", ("t", 2), ("t", 3))
    delta_far = jnp.concatenate([delta[2, 0:1], delta[3, 0:1]], axis=1)

    def second_pair(dz):
        here = rows(dz)
        dv, dk = pair_terms(1, here, delta_far)
        dv_acc[here] = dv_acc[here] + dv
        dk_acc[here] = dk_acc[here] + dk

    sums_of = {"dv": (dv_acc, dv_send, dv_recv), "dk": (dk_acc, dk_send, dk_recv)}

    def pass_on(*parts):
        for which in (LOW, HIGH):
            for kind, dz, way, first in parts:
                acc, out, recv = sums_of[kind]
                here = half(dz, which)
                value = acc[here]
                if not first:
                    arrived((kind, way, dz, which))
                    value = value + recv[here].astype(F32)
                out[here] = value.astype(BF16)
                target = (dz - way) % NZ
                landing = 4 if target == 0 and way == (1 if kind == "dv" else -1) else target
                send((kind, way, target, which), out.at[here], recv.at[half(landing, which)], at_z(way))

    def query_term(slot):
        return tn(ds[:, slot * ROWS:(slot + 1) * ROWS], kb[...])

    def query_pair(slot):
        dq_send[rows(slot - 2)] = query_term(slot).astype(BF16)

    second_pair(4)
    pass_on(("dv", 4, -1, True), ("dk", 4, 1, True))
    second_pair(5)
    second_pair(3)
    pass_on(("dk", 5, -1, True), ("dv", 3, 1, True))
    second_pair(2)
    second_pair(6)
    pass_on(("dv", 5, -1, False), ("dk", 3, 1, False))
    second_pair(7)
    second_pair(1)
    pass_on(("dk", 6, -1, False), ("dv", 2, 1, False))
    second_pair(0)
    query_pair(2)
    pass_on(("dv", 6, -1, False), ("dk", 2, 1, False))
    query_pair(3)
    send("dq pair", dq_send.at[pl.ds(0, 2 * ROWS)], dq_recv.at[pl.ds(0, 2 * ROWS)], pair_peer)
    pass_on(("dk", 7, -1, False), ("dv", 1, 1, False))
    dq_acc[rows(1)] = query_term(1)
    pass_on(("dv", 7, -1, False), ("dk", 1, 1, False))
    dq_acc[rows(0)] = query_term(0)
    arrived("dq pair")
    dq_send[rows(2)] = (dq_acc[rows(1)] + dq_recv[rows(1)].astype(F32)).astype(BF16)
    send("dq core", dq_send.at[rows(2)], dq_recv.at[rows(2)], core_peer)
    dq = dq_acc[rows(0)] + dq_recv[rows(0)].astype(F32)
    settle()
    arrived("dq core")
    dq_out[...] = (dq + dq_recv[rows(2)].astype(F32)).astype(BF16)

    def own(kind, acc, recv, out, which):
        arrived((kind, 1, 0, which), (kind, -1, 0, which))
        ahead, behind = recv[half(0, which)].astype(F32), recv[half(4, which)].astype(F32)
        out[half(0, which)] = (acc[half(0, which)] + ahead + behind).astype(BF16)

    for which in (LOW, HIGH):
        own("dv", dv_acc, dv_recv, dv_out, which)
        own("dk", dk_acc, dk_recv, dk_out, which)


def shards(queries, keys, values, saved_out, d_layer, out_weight, prefix, block_order):
    block = jax.ShapeDtypeStruct((ROWS, HD), BF16)
    anywhere = pl.BlockSpec(memory_space=pl.ANY)
    vmem = pl.BlockSpec(memory_space=pltpu.VMEM)
    operands = (block_order, queries, keys, values, saved_out, d_layer, out_weight)
    results = pl.pallas_call(
        kernel,
        out_shape=jax.ShapeDtypeStruct((3, ROWS, HD), BF16),
        in_specs=[pl.BlockSpec(memory_space=pltpu.SMEM)] + [anywhere] * 7,
        out_specs=vmem,
        scratch_shapes=[
            pltpu.SMEM((2 * NZ * NJ,), jnp.int32),
            pltpu.VMEM((NJ * ROWS, HD), BF16),
            pltpu.VMEM((NZ * ROWS, HD), BF16),
            pltpu.VMEM((NZ * ROWS, HD), BF16),
            pltpu.VMEM((ROWS, HD), BF16),
            pltpu.VMEM((NH * NH * ROWS, HD), BF16),
            pltpu.VMEM((HD, NH * NH * HD), BF16),
            pltpu.VMEM((NJ * ROWS, HD), BF16),
            pltpu.VMEM((NZ, NJ * ROWS), F32),
            pltpu.VMEM((NZ, NJ * ROWS), F32),
            pltpu.VMEM((4, 8, NJ * ROWS), F32),
            pltpu.VMEM((NJ, 8, ROWS), F32),
            pltpu.VMEM((NZ * ROWS, NJ * ROWS), F32),
            pltpu.VMEM((NZ * ROWS, NJ * ROWS), BF16),
            pltpu.VMEM((NZ * ROWS, NJ * ROWS), BF16),
            pltpu.VMEM((NZ * ROWS, HD), F32),
            pltpu.VMEM((NZ * ROWS, HD), F32),
            pltpu.VMEM((2 * ROWS, HD), F32),
            pltpu.VMEM((NZ * ROWS, HD), BF16),
            pltpu.VMEM((NZ * ROWS, HD), BF16),
            pltpu.VMEM((NZ * ROWS, HD), BF16),
            pltpu.VMEM((NZ * ROWS, HD), BF16),
            pltpu.VMEM((3 * ROWS, HD), BF16),
            pltpu.VMEM((3 * ROWS, HD), BF16),
            pltpu.SemaphoreType.DMA((7,)),
            pltpu.SemaphoreType.DMA((MESSAGES,)),
            pltpu.SemaphoreType.DMA((MESSAGES,)),
        ],
        compiler_params=pltpu.CompilerParams(
            collective_id=0, has_side_effects=True, vmem_limit_bytes=48 * 1024 * 1024
        ),
    )(prefix, *[pltpu.with_memory_space_constraint(operand, pltpu.HBM) for operand in operands])
    return results[0], results[1], results[2]


def solution(mesh):
    tokens = P("blk", "head")
    return jax.shard_map(
        shards,
        mesh=mesh,
        in_specs=(tokens, tokens, tokens, tokens, tokens, P("head", None), P(), P()),
        out_specs=(tokens, tokens, tokens),
        check_vma=False,
    )
```

```python
import functools

import jax
import jax.numpy as jnp
from jax import lax
from jax.experimental import pallas as pl
from jax.experimental.pallas import tpu as pltpu
from jax.sharding import PartitionSpec as P

MESH = pl.DeviceIdType.MESH
F32 = jnp.float32
BF16 = jnp.bfloat16

HD = 256
ROWS = 128
HALF = ROWS // 2
NZ = 8
NJ = 4
NH = 4
FLOOR = -1e30
SCALE = HD ** -0.5
MESSAGES = 100


def nt(a, b):
    return lax.dot_general(a, b, (((1,), (1,)), ((), ())), preferred_element_type=F32)


def nn(a, b):
    return lax.dot_general(a, b, (((1,), (0,)), ((), ())), preferred_element_type=F32)


def tn(a, b):
    return lax.dot_general(a, b, (((0,), (0,)), ((), ())), preferred_element_type=F32)


def rows(slot, count=ROWS, first=0):
    return pl.ds(slot * ROWS + first, count)


def kernel(
    prefix_ref,
    order_hbm,
    q_hbm,
    k_hbm,
    v_hbm,
    o_hbm,
    d_hbm,
    w_hbm,
    out,
    order_ref,
    qb,
    kb,
    vb,
    ob,
    dl,
    wb,
    gb,
    tops,
    sums,
    st,
    delta,
    score,
    prob,
    ds,
    dv_acc,
    dk_acc,
    dq_acc,
    dv_send,
    dk_send,
    dv_recv,
    dk_recv,
    dq_send,
    dq_recv,
    local_sem,
    send_sem,
    recv_sem,
):
    dq_out, dk_out, dv_out = out.at[0], out.at[1], out.at[2]
    blk = lax.axis_index("blk")
    head = lax.axis_index("head")
    z, j = lax.div(blk, NJ), lax.rem(blk, NJ)
    yh, x = lax.div(head, NH), lax.rem(head, NH)

    def at_z(step):
        return (lax.rem(z + (step + NZ), NZ) * NJ + j, head)

    def at_y(step):
        return (blk, lax.rem(yh + (step + NH), NH) * NH + x)

    def at_x(step):
        return (blk, yh * NH + lax.rem(x + (step + NH), NH))

    core_peer = (z * NJ + j + 1 - 2 * lax.rem(j, 2), head)
    pair_peer = (z * NJ + j + 2 - 4 * lax.div(j, 2), head)
    far_peer = (z * NJ + NJ - 1 - j, head)

    barrier = pltpu.get_barrier_semaphore()
    neighbours = (at_z(1), at_z(-1), at_y(1), at_y(-1), at_x(1), at_x(-1), core_peer, pair_peer, far_peer)
    for device in neighbours:
        pl.semaphore_signal(barrier, inc=1, device_id=device, device_id_type=MESH)

    loads = {}

    def load(name, src, dst):
        copy = pltpu.make_async_copy(src, dst, local_sem.at[len(loads)])
        copy.start()
        loads[name] = copy

    load("d", d_hbm, dl.at[rows(0)])
    load("k", k_hbm, kb.at[rows(0)])
    load("q", q_hbm, qb.at[rows(0)])
    load("v", v_hbm, vb.at[rows(0)])
    load("order", order_hbm, order_ref)
    load("w", w_hbm, wb)
    load("o", o_hbm, ob)
    for name in ("d", "k", "q", "v"):
        loads[name].wait()
    pl.semaphore_wait(barrier, len(neighbours))

    sent = {}
    unfinished = []

    def send(name, src, dst, device):
        index = len(sent)
        copy = pltpu.make_async_remote_copy(
            src_ref=src,
            dst_ref=dst,
            send_sem=send_sem.at[index],
            recv_sem=recv_sem.at[index],
            device_id=device,
            device_id_type=MESH,
        )
        copy.start()
        sent[name] = copy
        unfinished.append(copy)

    taken = set()

    def arrived(*names):
        for name in names:
            if name not in taken:
                taken.add(name)
                sent[name].wait_recv()

    def settle():
        while unfinished:
            unfinished.pop().wait_send()

    LOW, HIGH = 0, 1

    def half(slot, which):
        return rows(slot, HALF, which * HALF)

    def slot_of(dy, dx):
        return (dy % NH) * NH + dx % NH

    def y_start(which, way):
        send(("y", way, which), dl.at[half(0, which)], dl.at[half(slot_of(-way, 0), which)], at_y(way))

    def x_start(dy, which, way):
        block = half(slot_of(dy, 0), which)
        send(("x", way, dy, which), dl.at[block], dl.at[half(slot_of(dy, -way), which)], at_x(way))

    def x_both(dy, which):
        x_start(dy, which, 1 if which == LOW else -1)
        x_start(dy, which, -1 if which == LOW else 1)

    def y_relay(way):
        which = LOW if way == 1 else HIGH
        arrived(("y", way, which))
        send(("yy", way), dl.at[half(slot_of(-way, 0), which)], dl.at[half(slot_of(2, 0), which)], at_y(way))
        x_both((-way) % NH, which)

    def y_rest(way):
        which = HIGH if way == 1 else LOW
        arrived(("y", way, which))
        x_both((-way) % NH, which)

    def y_far(way):
        arrived(("yy", way))
        x_both(2, LOW if way == 1 else HIGH)

    def x_relay(dy, way):
        which = LOW if way == 1 else HIGH
        arrived(("x", way, dy, which))
        send(("xx", way, dy), dl.at[half(slot_of(dy, -way), which)], dl.at[half(slot_of(dy, 2), which)], at_x(way))

    stores = {"k": kb, "v": vb}

    def z_send(kind, step, way, which, src):
        near = (-way * step) % NZ
        send((kind, way, step, which), src, stores[kind].at[half((near - way) % NZ, which)], at_z(way))

    def z_start(kind, which):
        own = stores[kind]
        z_send(kind, 0, 1, which, own.at[half(0, which)])
        z_send(kind, 0, -1, 1 - which, own.at[half(0, 1 - which)])

    def z_relay(kind, step, way, which):
        arrived((kind, way, step - 1, which))
        z_send(kind, step, way, which, stores[kind].at[half((-way * step) % NZ, which)])

    y_start(LOW, 1)
    y_start(HIGH, -1)
    z_start("k", LOW)
    send("q pair", qb.at[rows(0)], qb.at[rows(2)], pair_peer)
    x_both(0, LOW)
    x_both(0, HIGH)
    z_start("k", HIGH)
    y_start(HIGH, 1)
    y_start(LOW, -1)
    send("q core", qb.at[rows(0)], qb.at[rows(1)], core_peer)
    z_start("v", LOW)

    loads["order"].wait()
    lane = lax.broadcasted_iota(jnp.int32, (1, ROWS), 1)
    sub = lax.broadcasted_iota(jnp.int32, (ROWS, 1), 0)

    def block_positions(index, iota):
        first, second = order_ref[2 * index], order_ref[2 * index + 1]
        return jnp.where(iota < HALF, first * HALF + iota, second * HALF + iota - HALF)

    group = (
        blk,
        z * NJ + j + 1 - 2 * lax.rem(j, 2),
        z * NJ + j + 2 - 4 * lax.div(j, 2),
        z * NJ + 3 - j,
    )
    reach = jnp.concatenate([block_positions(member, lane) for member in group], axis=1)
    reach = jnp.maximum(reach, prefix_ref[0] - 1)

    def key_arrival(kind, dz):
        if dz == 0:
            return ()
        if dz == NZ // 2:
            return (kind, 1, 3, LOW), (kind, -1, 3, HIGH)
        way, step = (1, NZ - 1 - dz) if dz > NZ // 2 else (-1, dz - 1)
        return (kind, way, step, LOW), (kind, way, step, HIGH)

    def score_block(dz):
        arrived(*key_arrival("k", dz))
        scores = nt(kb[rows(dz)], qb[...]) * SCALE
        key_pos = block_positions(lax.rem(z + dz, NZ) * NJ + j, sub)
        scores = jnp.where(key_pos <= reach, scores, FLOOR)
        top = jnp.max(scores, axis=0, keepdims=True)
        weights = jnp.exp(scores - top)
        score[rows(dz)] = weights
        tops[dz:dz + 1] = top
        sums[dz:dz + 1] = jnp.sum(weights, axis=0, keepdims=True)

    def arrival(dy, dx):
        if dx == 2:
            return ("xx", 1, dy), ("xx", -1, dy)
        if dx:
            way = 1 if dx == 3 else -1
            return ("x", way, dy, LOW), ("x", way, dy, HIGH)
        return ()

    def project(dy, dx):
        arrived(*arrival(dy, dx))
        source = lax.rem(yh + dy, NH) * NH + lax.rem(x + dx, NH)
        columns = pl.ds(pl.multiple_of(source * HD, HD), HD)
        return nt(dl[rows(slot_of(dy, dx))], wb[:, columns])

    def offer():
        top = jnp.max(tops[...], axis=0, keepdims=True)
        total = jnp.sum(sums[...] * jnp.exp(tops[...] - top), axis=0, keepdims=True)
        wide = (4, NJ * ROWS)
        st[0] = jnp.concatenate([jnp.broadcast_to(top, wide), jnp.broadcast_to(total, wide)], axis=0)
        for distance, device in ((2, pair_peer), (3, far_peer), (1, core_peer)):
            send(("s", distance), st.at[0], st.at[distance], device)

    def statistics(distance, row):
        found = st[distance, row:row + 1]
        parts = [found[:, (member ^ distance) * ROWS:((member ^ distance) + 1) * ROWS] for member in range(NJ)]
        return jnp.concatenate(parts, axis=1)

    def merge():
        arrived(("s", 1), ("s", 2), ("s", 3))
        part_tops = [statistics(distance, 0) for distance in range(NJ)]
        top = functools.reduce(jnp.maximum, part_tops)
        total = sum(statistics(distance, 4) * jnp.exp(part_tops[distance] - top) for distance in range(NJ))
        tops[...] = jnp.exp(tops[...] - (top + jnp.log(total)))

    loads["w"].wait()
    grad = project(0, 0)
    z_relay("k", 1, 1, LOW)
    z_relay("k", 1, -1, HIGH)
    x_relay(0, 1)
    z_relay("k", 1, 1, HIGH)
    z_relay("k", 1, -1, LOW)
    x_relay(0, -1)
    z_start("v", HIGH)
    grad = grad + project(0, 3)
    grad = grad + project(0, 1)
    y_relay(1)
    y_relay(-1)
    z_relay("k", 2, 1, LOW)
    z_relay("k", 2, -1, HIGH)
    y_rest(1)
    y_rest(-1)
    grad = grad + project(3, 0)
    grad = grad + project(1, 0)
    z_relay("k", 2, 1, HIGH)
    z_relay("k", 2, -1, LOW)
    arrived("q pair")
    send("q on", qb.at[rows(2)], qb.at[rows(3)], core_peer)
    z_relay("v", 1, 1, LOW)
    z_relay("v", 1, -1, HIGH)
    grad = grad + project(0, 2)
    x_relay(3, 1)
    x_relay(1, -1)
    arrived("q core", "q on")
    score_block(0)
    score_block(1)
    score_block(7)
    z_relay("k", 3, 1, LOW)
    z_relay("k", 3, -1, HIGH)
    z_relay("v", 1, 1, HIGH)
    z_relay("v", 1, -1, LOW)
    y_far(1)
    y_far(-1)
    score_block(2)
    score_block(6)
    grad = grad + project(2, 0)
    grad = grad + project(3, 3)
    x_relay(3, -1)
    grad = grad + project(3, 1)
    x_relay(1, 1)
    score_block(3)
    score_block(5)
    grad = grad + project(1, 3)
    grad = grad + project(1, 1)
    z_relay("v", 2, 1, LOW)
    z_relay("v", 2, -1, HIGH)
    x_relay(2, 1)
    score_block(4)
    offer()
    z_relay("v", 2, 1, HIGH)
    z_relay("v", 2, -1, LOW)
    x_relay(2, -1)
    z_relay("v", 3, 1, LOW)
    z_relay("v", 3, -1, HIGH)
    grad = grad + project(2, 3)
    grad = grad + project(2, 1)
    grad = grad + project(1, 2)
    grad = grad + project(3, 2)
    grad = grad + project(2, 2)
    grad_low = grad.astype(BF16)
    gb[rows(0)] = grad_low
    send("g pair", gb.at[rows(0)], gb.at[rows(2)], pair_peer)
    send("g core", gb.at[rows(0)], gb.at[rows(1)], core_peer)
    loads["o"].wait()
    products = grad_low.astype(F32) * ob[...].astype(F32)
    ones = jnp.ones((8, HD), F32)
    delta[0] = lax.dot_general(
        ones, products, (((1,), (1,)), ((), ())), precision=lax.Precision.HIGHEST, preferred_element_type=F32
    )
    for distance, device in ((2, pair_peer), (3, far_peer), (1, core_peer)):
        send(("t", distance), delta.at[0], delta.at[distance], device)
    merge()

    def make_prob(dz):
        probs = score[rows(dz)] * tops[dz:dz + 1]
        score[rows(dz)] = probs
        prob[rows(dz)] = probs.astype(BF16)

    for dz in range(NZ):
        make_prob(dz)
    for dz in range(NZ):
        arrived(*key_arrival("v", dz))

    def pair_terms(pair, here, delta_row):
        columns = pl.ds(2 * ROWS * pair, 2 * ROWS)
        grad_pair = gb[columns]
        grad_probs = nt(vb[here], grad_pair)
        grad_scores = (score[here, columns] * (grad_probs - delta_row) * SCALE).astype(BF16)
        ds[here, columns] = grad_scores
        return nn(prob[here, columns], grad_pair), nn(grad_scores, qb[columns])

    arrived("g core", ("t", 1))
    delta_row = jnp.concatenate([delta[0, 0:1], delta[1, 0:1]], axis=1)

    def first_pair(dz):
        here = rows(dz)
        dv, dk = pair_terms(0, here, delta_row)
        dv_acc[here] = dv
        dk_acc[here] = dk

    for dz in (4, 5, 3, 6):
        first_pair(dz)
    arrived("g pair")
    send("g on", gb.at[rows(2)], gb.at[rows(3)], core_peer)
    for dz in (2, 7, 1, 0):
        first_pair(dz)
    arrived("g on", ("t", 2), ("t", 3))
    delta_far = jnp.concatenate([delta[2, 0:1], delta[3, 0:1]], axis=1)

    def second_pair(dz):
        here = rows(dz)
        dv, dk = pair_terms(1, here, delta_far)
        dv_acc[here] = dv_acc[here] + dv
        dk_acc[here] = dk_acc[here] + dk

    sums_of = {"dv": (dv_acc, dv_send, dv_recv), "dk": (dk_acc, dk_send, dk_recv)}

    def pass_on(*parts):
        for which in (LOW, HIGH):
            for kind, dz, way, first in parts:
                acc, out, recv = sums_of[kind]
                here = half(dz, which)
                value = acc[here]
                if not first:
                    arrived((kind, way, dz, which))
                    value = value + recv[here].astype(F32)
                out[here] = value.astype(BF16)
                target = (dz - way) % NZ
                landing = 4 if target == 0 and way == (1 if kind == "dv" else -1) else target
                send((kind, way, target, which), out.at[here], recv.at[half(landing, which)], at_z(way))

    def query_term(slot):
        return tn(ds[:, slot * ROWS:(slot + 1) * ROWS], kb[...])

    def query_pair(slot):
        dq_send[rows(slot - 2)] = query_term(slot).astype(BF16)

    second_pair(4)
    pass_on(("dv", 4, -1, True), ("dk", 4, 1, True))
    second_pair(5)
    second_pair(3)
    pass_on(("dk", 5, -1, True), ("dv", 3, 1, True))
    second_pair(2)
    second_pair(6)
    pass_on(("dv", 5, -1, False), ("dk", 3, 1, False))
    second_pair(7)
    second_pair(1)
    pass_on(("dk", 6, -1, False), ("dv", 2, 1, False))
    second_pair(0)
    query_pair(2)
    pass_on(("dv", 6, -1, False), ("dk", 2, 1, False))
    query_pair(3)
    send("dq pair", dq_send.at[pl.ds(0, 2 * ROWS)], dq_recv.at[pl.ds(0, 2 * ROWS)], pair_peer)
    pass_on(("dk", 7, -1, False), ("dv", 1, 1, False))
    dq_acc[rows(1)] = query_term(1)
    pass_on(("dv", 7, -1, False), ("dk", 1, 1, False))
    dq_acc[rows(0)] = query_term(0)
    arrived("dq pair")
    dq_send[rows(2)] = (dq_acc[rows(1)] + dq_recv[rows(1)].astype(F32)).astype(BF16)
    send("dq core", dq_send.at[rows(2)], dq_recv.at[rows(2)], core_peer)
    dq = dq_acc[rows(0)] + dq_recv[rows(0)].astype(F32)
    settle()
    arrived("dq core")
    dq_out[...] = (dq + dq_recv[rows(2)].astype(F32)).astype(BF16)

    def own(kind, acc, recv, out, which):
        arrived((kind, 1, 0, which), (kind, -1, 0, which))
        ahead, behind = recv[half(0, which)].astype(F32), recv[half(4, which)].astype(F32)
        out[half(0, which)] = (acc[half(0, which)] + ahead + behind).astype(BF16)

    for which in (LOW, HIGH):
        own("dv", dv_acc, dv_recv, dv_out, which)
        own("dk", dk_acc, dk_recv, dk_out, which)


def shards(queries, keys, values, saved_out, d_layer, out_weight, prefix, block_order):
    block = jax.ShapeDtypeStruct((ROWS, HD), BF16)
    anywhere = pl.BlockSpec(memory_space=pl.ANY)
    vmem = pl.BlockSpec(memory_space=pltpu.VMEM)
    operands = (block_order, queries, keys, values, saved_out, d_layer, out_weight)
    results = pl.pallas_call(
        kernel,
        out_shape=jax.ShapeDtypeStruct((3, ROWS, HD), BF16),
        in_specs=[pl.BlockSpec(memory_space=pltpu.SMEM)] + [anywhere] * 7,
        out_specs=vmem,
        scratch_shapes=[
            pltpu.SMEM((2 * NZ * NJ,), jnp.int32),
            pltpu.VMEM((NJ * ROWS, HD), BF16),
            pltpu.VMEM((NZ * ROWS, HD), BF16),
            pltpu.VMEM((NZ * ROWS, HD), BF16),
            pltpu.VMEM((ROWS, HD), BF16),
            pltpu.VMEM((NH * NH * ROWS, HD), BF16),
            pltpu.VMEM((HD, NH * NH * HD), BF16),
            pltpu.VMEM((NJ * ROWS, HD), BF16),
            pltpu.VMEM((NZ, NJ * ROWS), F32),
            pltpu.VMEM((NZ, NJ * ROWS), F32),
            pltpu.VMEM((4, 8, NJ * ROWS), F32),
            pltpu.VMEM((NJ, 8, ROWS), F32),
            pltpu.VMEM((NZ * ROWS, NJ * ROWS), F32),
            pltpu.VMEM((NZ * ROWS, NJ * ROWS), BF16),
            pltpu.VMEM((NZ * ROWS, NJ * ROWS), BF16),
            pltpu.VMEM((NZ * ROWS, HD), F32),
            pltpu.VMEM((NZ * ROWS, HD), F32),
            pltpu.VMEM((2 * ROWS, HD), F32),
            pltpu.VMEM((NZ * ROWS, HD), BF16),
            pltpu.VMEM((NZ * ROWS, HD), BF16),
            pltpu.VMEM((NZ * ROWS, HD), BF16),
            pltpu.VMEM((NZ * ROWS, HD), BF16),
            pltpu.VMEM((3 * ROWS, HD), BF16),
            pltpu.VMEM((3 * ROWS, HD), BF16),
            pltpu.SemaphoreType.DMA((7,)),
            pltpu.SemaphoreType.DMA((MESSAGES,)),
            pltpu.SemaphoreType.DMA((MESSAGES,)),
        ],
        compiler_params=pltpu.CompilerParams(
            collective_id=0, has_side_effects=True, vmem_limit_bytes=48 * 1024 * 1024
        ),
    )(prefix, *[pltpu.with_memory_space_constraint(operand, pltpu.HBM) for operand in operands])
    return results[0], results[1], results[2]


def solution(mesh):
    tokens = P("blk", "head")
    return jax.shard_map(
        shards,
        mesh=mesh,
        in_specs=(tokens, tokens, tokens, tokens, tokens, P("head", None), P(), P()),
        out_specs=(tokens, tokens, tokens),
        check_vma=False,
    )
```
